32 devices in a mesh: dp: 8 (over z, x), cent: 4 (over y, core).
Axes of the slice: x: 2, y: 2, z: 4, core: 2. Of those that a mesh axis runs over, the one named last changes fastest.
Arguments:
- embeddings: bfloat16 [8192, 4096], P('dp'), may hold values from -15 to 15
- centroids: bfloat16 [8192, 4096], P('cent', 'dp'), may hold values from -12 to 12
Outputs:
- shares: bfloat16 [8192, 8192], P('dp', 'cent')
- new_centroids: bfloat16 [8192, 4096], P('cent', 'dp')
The draws below stay inside these ranges and needn't reach their ends.
All inputs are finite; a program needn't handle non-finite values.
Results may differ from the reference program's by a relative error of at most 0.0034.
Values may be sent and summed in bfloat16 or wider, within the bound.
A program may use at most 128 MiB of HBM per device.

```python
import jax
import jax.numpy as jnp
from jax import lax

D = 4096
K = 8192
ROUNDS = 3
TOKENS = 8192


def group_count():
    return max(4, min(64, K // 128))


def shared_means(key):
    return jnp.clip(jax.random.normal(key, (group_count(), D), jnp.float32), -5.0, 5.0)


def draw_embeddings(key, part):
    means = shared_means(key)
    key = jax.random.fold_in(key, 11)
    key_group, key_strength, key_noise = jax.random.split(key, 3)
    group_ids = jax.random.randint(key_group, (TOKENS,), 0, group_count())
    strength = jax.random.uniform(key_strength, (TOKENS, 1), jnp.float32, 0.5, 1.5)
    centre = strength * means[group_ids]
    noise = jnp.clip(jax.random.normal(key_noise, (TOKENS, D), jnp.float32), -6.0, 6.0)
    values = centre + noise
    return values.astype(jnp.bfloat16)


def draw_centroids(key, part):
    means = shared_means(key)
    key = jax.random.fold_in(key, 23)
    key_pick, key_count, key_mix, key_noise = jax.random.split(key, 4)
    picks = jax.random.randint(key_pick, (K, 4), 0, group_count())
    count = jax.random.randint(key_count, (K, 1), 2, 5)
    used = (jnp.arange(4)[None, :] < count).astype(jnp.float32)
    mixing = jax.random.uniform(key_mix, (K, 4), jnp.float32, 0.2, 1.0) * used
    mixing = mixing / jnp.sum(mixing, 1, keepdims=True)
    centre = jnp.zeros((K, D), jnp.float32)
    for slot in range(4):
        centre = centre + mixing[:, slot:slot + 1] * means[picks[:, slot]]
    noise = 0.7 * jnp.clip(jax.random.normal(key_noise, (K, D), jnp.float32), -6.0, 6.0)
    return (centre + noise).astype(jnp.bfloat16)


def setup_inputs(seed: int = 0) -> dict:
    seeds = jax.random.split(jax.random.key(seed), 3)
    embeddings = draw_embeddings(jax.random.fold_in(seeds[2], 71), 0)
    centroids = draw_centroids(jax.random.fold_in(seeds[2], 71), 0)
    return {"embeddings": embeddings, "centroids": centroids}


def reference(embeddings, centroids):
    rows_float = embeddings.astype(jnp.float32)
    normed = (rows_float * lax.rsqrt(lax.optimization_barrier(jnp.sum(rows_float * rows_float, 1, keepdims=True)) + 1e-06)).astype(jnp.bfloat16)
    cent_float = centroids.astype(jnp.float32)
    scale = lax.rsqrt(lax.optimization_barrier(jnp.sum(cent_float * cent_float, 1)) + 1e-06)
    scores = jnp.dot(normed, centroids.T, preferred_element_type=jnp.float32) * scale[None, :]
    weights = jnp.exp(scores * 20.0)
    target = TOKENS / K
    for sweep in range(ROUNDS):
        weights = weights * (target / lax.optimization_barrier(jnp.sum(weights, 0)))[None, :]
        weights = weights / lax.optimization_barrier(jnp.sum(weights, 1, keepdims=True))
    shares = weights.astype(jnp.bfloat16)
    col_mass = lax.optimization_barrier(jnp.sum(shares.astype(jnp.float32), 0))
    sums = jnp.dot(shares.T, embeddings, preferred_element_type=jnp.float32)
    new_centroids = (sums / col_mass[:, None]).astype(jnp.bfloat16)
    return (shares, new_centroids)
```

```python
import functools

import jax
import jax.numpy as jnp
from jax import lax
from jax.experimental import pallas as pl
from jax.experimental.pallas import tpu as pltpu
from jax.sharding import PartitionSpec as P

ROUNDS = 3
LINE = 4
MESH = pl.DeviceIdType.MESH
F32 = jnp.float32
BF16 = jnp.bfloat16


def arrival_order(n, na, nb):
    table = []
    for me in range(n):
        a, b = divmod(me, nb)
        table.append(
            sorted(
                range(n),
                key=lambda s: (abs(s // nb - a) + abs(s % nb - b), abs(s % nb - b), s),
            )
        )
    return table


def pick(me, values):
    out = jnp.int32(values[0])
    for i, v in enumerate(values[1:], 1):
        out = jnp.where(me == i, jnp.int32(v), out)
    return out


def scores_kernel(
    n, nc, target, emb, cent, shares, mass, e_x, e_v, gath, w, sq, pr, rexp,
    col_out, col_in, row_out, row_in, loc_sem, snd, rcv, csnd, crcv, rsnd, rrcv,
    esnd, ercv, fsnd, frcv,
):
    me = lax.axis_index("dp")
    mc = lax.axis_index("cent")
    na = min(LINE, n)
    nb = n // na
    a, b = me // nb, me % nb
    rows = e_v.shape[0]
    local_k, feats = cent.shape
    half_k = local_k // 2
    tile = min(256, half_k)
    lanes = local_k // 128

    barrier = pltpu.get_barrier_semaphore()
    for k in range(1, n):
        pl.semaphore_signal(barrier, inc=1, device_id={"dp": lax.rem(me + k, n)}, device_id_type=MESH)
    for k in range(1, nc):
        pl.semaphore_signal(barrier, inc=1, device_id={"cent": lax.rem(mc + k, nc)}, device_id_type=MESH)
    pl.semaphore_wait(barrier, n - 1 + nc - 1)

    order = arrival_order(n, na, nb)

    def sends(e, src, h):
        sa, sb = src // nb, src % nb
        da, db = sa - a, sb - b
        ref = (cent if e == 0 else gath.at[src]).at[pl.ds(pl.multiple_of(h * half_k, half_k), half_k)]
        dst = gath.at[src].at[pl.ds(pl.multiple_of(h * half_k, half_k), half_k)]
        conds = (
            ((db == 0) & (da <= 0) & (a < na - 1), me + nb),
            ((db == 0) & (da >= 0) & (a > 0), me - nb),
            ((db <= 0) & (b < nb - 1), me + 1),
            ((db >= 0) & (b > 0), me - 1),
        )
        out = []
        for i, (cond, to) in enumerate(conds):
            out.append((cond, pltpu.make_async_remote_copy(
                src_ref=ref, dst_ref=dst, send_sem=snd.at[e, i, h], recv_sem=rcv.at[src, h],
                device_id={"dp": to}, device_id_type=MESH)))
        return out

    for h in range(2):
        for cond, copy in sends(0, me, h):
            @pl.when(cond)
            def _():
                copy.start()
    e_copy = pltpu.make_async_copy(emb, e_v, loc_sem.at[0])
    e_copy.start()
    own = pltpu.make_async_copy(cent, gath.at[me], loc_sem.at[1])
    own.start()
    e_copy.wait()

    chunk = 16

    @pl.loop(0, rows // chunk)
    def _(i):
        at = pl.ds(pl.multiple_of(i * chunk, chunk), chunk)
        x = e_v[at, :].astype(F32)
        s = jnp.sum(x * x, axis=1, keepdims=True)
        e_v[at, :] = (x * lax.rsqrt(s + 1e-06)).astype(BF16)

    own.wait()
    sq[...] = jnp.zeros_like(sq)
    ones = jnp.ones((8, feats), BF16)
    nt = (((1,), (1,)), ((), ()))

    for e in range(n):
        src = me if e == 0 else pick(me, [order[d][e] for d in range(n)])
        fcols = pl.ds(pl.multiple_of(src * feats, feats), feats)

        @pl.loop(0, 2)
        def _(h):
            if e > 0:
                outs = sends(e, src, h)
                outs[0][1].wait_recv()
                for cond, copy in outs:
                    @pl.when(cond)
                    def _():
                        copy.start()

            @pl.loop(0, half_k // tile)
            def _(t):
                k0 = pl.multiple_of(h * half_k + t * tile, tile)
                block = gath[src, pl.ds(k0, tile), :]
                part = lax.dot_general(e_v[:, fcols], block, nt, preferred_element_type=F32)
                if e == 0:
                    w[:, pl.ds(k0, tile)] = part
                else:
                    w[:, pl.ds(k0, tile)] += part
                bf = block.astype(F32)
                b2 = bf * bf
                hi = b2.astype(BF16)
                lo = (b2 - hi.astype(F32)).astype(BF16)
                sq[:, pl.ds(k0, tile)] += lax.dot_general(
                    ones, hi, nt, preferred_element_type=F32
                ) + lax.dot_general(ones, lo, nt, preferred_element_type=F32)

    half_rows = rows // 2
    mine = pl.ds(pl.multiple_of(lax.rem(mc, 2) * half_rows, half_rows), half_rows)
    e_copies, f_copies = [], []
    for k in range(1, nb):
        b2 = lax.rem(b + k, nb)
        for q in range(na):
            cols = pl.ds(pl.multiple_of((q * nb + b2) * feats, feats), feats)
            c = pltpu.make_async_remote_copy(
                src_ref=emb.at[mine, cols], dst_ref=e_x.at[k - 1, mine, pl.ds(q * feats, feats)],
                send_sem=esnd.at[k, q], recv_sem=ercv.at[k, q],
                device_id={"dp": a * nb + b2}, device_id_type=MESH)
            c.start()
            e_copies.append(c)
        f_copies.append(pltpu.make_async_remote_copy(
            src_ref=e_x.at[k - 1, mine], dst_ref=e_x.at[k - 1, mine],
            send_sem=fsnd.at[k], recv_sem=frcv.at[k],
            device_id={"cent": mc + 1 - 2 * lax.rem(mc, 2)}, device_id_type=MESH))

    def exchange_cols(r, part8):
        col_out[r] = jnp.sum(part8, axis=0, keepdims=True)
        copies = []
        for k in range(1, n):
            c = pltpu.make_async_remote_copy(
                src_ref=col_out.at[r], dst_ref=col_in.at[r, k], send_sem=csnd.at[r, k], recv_sem=crcv.at[r, k],
                device_id={"dp": lax.rem(me + k, n)}, device_id_type=MESH)
            c.start()
            copies.append(c)
        total = col_out[r]
        for k, c in enumerate(copies, 1):
            c.wait()
            total = total + col_in[r, k]
        return total

    def exchange_rows(r):
        for k in range(rows // 128):
            block = pr[k * 128:(k + 1) * 128, :]
            row_out[r, k:k + 1, :] = jnp.sum(block.T, axis=0, keepdims=True)
        copies = []
        for k in range(1, nc):
            c = pltpu.make_async_remote_copy(
                src_ref=row_out.at[r], dst_ref=row_in.at[r, k], send_sem=rsnd.at[r, k], recv_sem=rrcv.at[r, k],
                device_id={"cent": lax.rem(mc + k, nc)}, device_id_type=MESH)
            c.start()
            copies.append(c)
        total = row_out[r]
        for k, c in enumerate(copies, 1):
            c.wait()
            total = total + row_in[r, k]
        inv = 1.0 / total
        for k in range(rows // 128):
            rexp[k * 128:(k + 1) * 128, :] = jnp.broadcast_to(inv[k:k + 1, :], (128, 128)).T

    def wide(x):
        return jnp.concatenate([x] * lanes, axis=1)

    def narrow(x):
        out = x[:, :128]
        for t in range(1, lanes):
            out = out + x[:, t * 128:(t + 1) * 128]
        return out

    scale8 = lax.rsqrt(sq[...] + 1e-06) * 20.0
    zero8 = jnp.zeros((8, local_k), F32)

    def exp_pass(i, acc):
        at = pl.ds(pl.multiple_of(i * 8, 8), 8)
        x = jnp.exp(w[at, :] * scale8)
        w[at, :] = x
        return acc + x

    part8 = lax.fori_loop(0, rows // 8, exp_pass, zero8)
    for r in range(ROUNDS):
        if r > 0:
            def col_pass(i, acc):
                at = pl.ds(pl.multiple_of(i * 8, 8), 8)
                return acc + w[at, :] * wide(rexp[at, :])

            part8 = lax.fori_loop(0, rows // 8, col_pass, zero8)
        c8 = jnp.broadcast_to(target / exchange_cols(r, part8), (8, local_k))

        def row_pass(i, _):
            at = pl.ds(pl.multiple_of(i * 8, 8), 8)
            pr[at, :] = narrow(w[at, :] * c8)
            return 0

        lax.fori_loop(0, rows // 8, row_pass, 0)
        exchange_rows(r)

    for c in e_copies:
        c.wait()
    for c in f_copies:
        c.start()
    c16 = jnp.broadcast_to(c8[:1], (16, local_k))

    def share_pass(i, acc):
        at = pl.ds(pl.multiple_of(i * 16, 16), 16)
        s = (w[at, :] * wide(rexp[at, :]) * c16).astype(BF16)
        shares[at, :] = s
        s = s.astype(F32)
        return acc + (s[:8] + s[8:])

    part8 = lax.fori_loop(0, rows // 16, share_pass, zero8)
    mass[...] = exchange_cols(ROUNDS, part8)
    for c in f_copies:
        c.wait()

    for e in range(n):
        src = me if e == 0 else pick(me, [order[d][e] for d in range(n)])
        for h in range(2):
            for cond, copy in sends(e, src, h):
                @pl.when(cond)
                def _():
                    copy.wait_send()


def balanced(n, nc, embeddings, centroids):
    rows, width = embeddings.shape
    local_k, feats = centroids.shape
    target = rows * n / (local_k * nc)
    na = min(LINE, n)
    nb = n // na
    vmem = pl.BlockSpec(memory_space=pltpu.VMEM)
    dma = pltpu.SemaphoreType.DMA
    return pl.pallas_call(
        functools.partial(scores_kernel, n, nc, target),
        out_shape=(
            jax.ShapeDtypeStruct((rows, local_k), BF16),
            jax.ShapeDtypeStruct((1, local_k), F32),
            jax.ShapeDtypeStruct((nb - 1, rows, na * feats), BF16),
        ),
        in_specs=[pl.BlockSpec(memory_space=pl.ANY)] * 2,
        out_specs=(vmem, vmem, pl.BlockSpec(memory_space=pl.ANY)),
        scratch_shapes=[
            pltpu.VMEM((rows, width), BF16),
            pltpu.VMEM((n, local_k, feats), BF16),
            pltpu.VMEM((rows, local_k), F32),
            pltpu.VMEM((8, local_k), F32),
            pltpu.VMEM((rows, 128), F32),
            pltpu.VMEM((rows, 128), F32),
            pltpu.VMEM((ROUNDS + 1, 1, local_k), F32),
            pltpu.VMEM((ROUNDS + 1, n, 1, local_k), F32),
            pltpu.VMEM((ROUNDS, rows // 128, 128), F32),
            pltpu.VMEM((ROUNDS, nc, rows // 128, 128), F32),
            dma((2,)),
            dma((n, 4, 2)),
            dma((n, 2)),
            dma((ROUNDS + 1, n)),
            dma((ROUNDS + 1, n)),
            dma((ROUNDS, nc)),
            dma((ROUNDS, nc)),
            dma((nb, na)),
            dma((nb, na)),
            dma((nb,)),
            dma((nb,)),
        ],
        compiler_params=pltpu.CompilerParams(
            collective_id=0, has_side_effects=True, vmem_limit_bytes=58 * 2**20
        ),
        cost_estimate=pl.CostEstimate(
            flops=2 * rows * width * local_k, bytes_accessed=48 * 2**20, transcendentals=rows * local_k
        ),
    )(embeddings, centroids)


def means_kernel(
    n, chunk, emb, shares, mass, e_x, out, s_v, s_x, e_v, ex_v, st, slots, p_own, p_now,
    loc_sem, xsnd, xrcv, snd, rcv,
):
    me = lax.axis_index("dp")
    na = min(LINE, n)
    nb = n // na
    a, b = me // nb, me % nb
    rows, local_k = s_v.shape
    feats = out.shape[1]
    chunks = local_k // chunk

    barrier = pltpu.get_barrier_semaphore()
    for k in range(1, nb):
        pl.semaphore_signal(
            barrier, inc=1, device_id={"dp": a * nb + lax.rem(b + k, nb)}, device_id_type=MESH)

    @pl.when(a > 0)
    def _():
        pl.semaphore_signal(barrier, inc=1, device_id={"dp": me - nb}, device_id_type=MESH)

    @pl.when(a < na - 1)
    def _():
        pl.semaphore_signal(barrier, inc=1, device_id={"dp": me + nb}, device_id_type=MESH)

    neighbours = jnp.where(a > 0, 1, 0) + jnp.where(a < na - 1, 1, 0) + nb - 1
    pl.semaphore_wait(barrier, neighbours)

    def span(j):
        return pl.ds(pl.multiple_of(j * chunk, chunk), chunk)

    def share_copy(j, k):
        return pltpu.make_async_remote_copy(
            src_ref=shares.at[:, span(j)], dst_ref=s_x.at[k - 1, :, span(j)],
            send_sem=xsnd.at[j, k], recv_sem=xrcv.at[j, k],
            device_id={"dp": a * nb + lax.rem(b + k, nb)}, device_id_type=MESH)

    @pl.loop(0, chunks)
    def _(j):
        for k in range(1, nb):
            share_copy(j, k).start()

    loads = [pltpu.make_async_copy(shares, s_v, loc_sem.at[0]), pltpu.make_async_copy(e_x, ex_v, loc_sem.at[1])]
    for q in range(na):
        cols = pl.ds(pl.multiple_of((q * nb + b) * feats, feats), feats)
        loads.append(pltpu.make_async_copy(
            emb.at[:, cols], e_v.at[:, pl.ds(q * feats, feats)], loc_sem.at[2 + q]))
    for c in loads:
        c.start()
    for c in loads:
        c.wait()

    far_first = [sorted(range(na), key=lambda q: (-abs(q - m), q)) for m in range(na)]

    def up_copy(j, q):
        return pltpu.make_async_remote_copy(
            src_ref=slots.at[j, q], dst_ref=slots.at[j, q], send_sem=snd.at[j, q], recv_sem=rcv.at[j, q],
            device_id={"dp": me + nb}, device_id_type=MESH)

    def down_copy(j, q):
        to = jnp.where(q == a - 1, na, q)
        return pltpu.make_async_remote_copy(
            src_ref=slots.at[j, q], dst_ref=slots.at[j, to], send_sem=snd.at[j, q], recv_sem=rcv.at[j, to],
            device_id={"dp": me - nb}, device_id_type=MESH)

    def arrived(j, q):
        pltpu.make_async_remote_copy(
            src_ref=slots.at[j, q], dst_ref=slots.at[j, q], send_sem=snd.at[j, 0], recv_sem=rcv.at[j, q],
            device_id={"dp": me}, device_id_type=MESH).wait_recv()

    def send_chunk(j):
        for k in range(1, nb):
            share_copy(j, k).wait_recv()
        st[0] = s_v[:, span(j)].T
        for k in range(1, nb):
            st[k] = s_x[k - 1, :, span(j)].T
        for i in range(na):
            q = pick(a, [far_first[m][i] for m in range(na)])
            cols = pl.ds(pl.multiple_of(q * feats, feats), feats)
            p = jnp.dot(st[0], e_v[:, cols], preferred_element_type=F32)
            for k in range(1, nb):
                p = p + jnp.dot(st[k], ex_v[k - 1, :, cols], preferred_element_type=F32)
            if i == na - 1:
                p_own[j] = p
                continue
            p_now[...] = p
            up = q > a
            has_in = (up & (a > 0)) | ((q < a) & (a < na - 1))

            @pl.when(has_in)
            def _():
                arrived(j, q)
                p_now[...] += slots[j, q].astype(F32)

            slots[j, q] = p_now[...].astype(BF16)

            @pl.when(up)
            def _():
                up_copy(j, q).start()

            @pl.when(q < a)
            def _():
                down_copy(j, q).start()

    def finish_chunk(j):
        @pl.when(a > 0)
        def _():
            arrived(j, a)
            p_own[j] += slots[j, a].astype(F32)

        @pl.when(a < na - 1)
        def _():
            arrived(j, na)
            p_own[j] += slots[j, na].astype(F32)

        for t in range(chunk // 128):
            at = pl.ds(pl.multiple_of(j * chunk + t * 128, 128), 128)
            m = jnp.broadcast_to(mass[:, at], (128, 128)).T
            m = jnp.concatenate([m] * (feats // 128), axis=1)
            out[at, :] = (p_own[j, t * 128:(t + 1) * 128, :] / m).astype(BF16)

    late = min(2, chunks)

    @pl.loop(0, chunks)
    def _(j):
        send_chunk(j)

        @pl.when(j >= late)
        def _():
            finish_chunk(j - late)

    @pl.loop(chunks - late, chunks)
    def _(j):
        finish_chunk(j)

    @pl.loop(0, chunks)
    def _(j):
        for k in range(1, nb):
            share_copy(j, k).wait_send()
        for q in range(na):
            @pl.when(a < q)
            def _():
                up_copy(j, q).wait_send()

            @pl.when(a > q)
            def _():
                down_copy(j, q).wait_send()


def means(n, embeddings, shares, mass, e_x, feats):
    rows, local_k = shares.shape
    na = min(LINE, n)
    nb = n // na
    chunk = min(256, local_k)
    chunks = local_k // chunk
    vmem = pl.BlockSpec(memory_space=pltpu.VMEM)
    hbm = pl.BlockSpec(memory_space=pl.ANY)
    dma = pltpu.SemaphoreType.DMA
    return pl.pallas_call(
        functools.partial(means_kernel, n, chunk),
        out_shape=jax.ShapeDtypeStruct((local_k, feats), BF16),
        in_specs=[hbm, hbm, vmem, hbm],
        out_specs=vmem,
        scratch_shapes=[
            pltpu.VMEM((rows, local_k), BF16),
            pltpu.VMEM((nb - 1, rows, local_k), BF16),
            pltpu.VMEM((rows, na * feats), BF16),
            pltpu.VMEM((nb - 1, rows, na * feats), BF16),
            pltpu.VMEM((nb, chunk, rows), BF16),
            pltpu.VMEM((chunks, na + 1, chunk, feats), BF16),
            pltpu.VMEM((chunks, chunk, feats), F32),
            pltpu.VMEM((chunk, feats), F32),
            dma((2 + na,)),
            dma((chunks, nb)),
            dma((chunks, nb)),
            dma((chunks, na)),
            dma((chunks, na + 1)),
        ],
        compiler_params=pltpu.CompilerParams(
            collective_id=1, has_side_effects=True, vmem_limit_bytes=58 * 2**20
        ),
        cost_estimate=pl.CostEstimate(
            flops=2 * rows * n * feats * local_k, bytes_accessed=24 * 2**20, transcendentals=0
        ),
    )(embeddings, shares, mass, e_x)


def on_device(n, nc, embeddings, centroids):
    shares, mass, e_x = balanced(n, nc, embeddings, centroids)
    new_centroids = means(n, embeddings, shares, mass, e_x, centroids.shape[1])
    return (shares, new_centroids)


def solution(mesh):
    in_specs = (P("dp", None), P("cent", "dp"))
    out_specs = (P("dp", "cent"), P("cent", "dp"))
    return jax.shard_map(
        functools.partial(on_device, mesh.shape["dp"], mesh.shape["cent"]),
        mesh=mesh, in_specs=in_specs, out_specs=out_specs, check_vma=False,
    )
```

```python
import functools

import jax
import jax.numpy as jnp
from jax import lax
from jax.experimental import pallas as pl
from jax.experimental.pallas import tpu as pltpu
from jax.sharding import PartitionSpec as P

ROUNDS = 3
LINE = 4
PIECES = 4
DETOUR = 3
MESH = pl.DeviceIdType.MESH
F32 = jnp.float32
BF16 = jnp.bfloat16


def detour(a, na):
    if isinstance(a, int):
        return a + 1 if a < na // 2 else a - 1
    return jnp.where(a < na // 2, a + 1, a - 1)


def arrival_order(n, na, nb):
    table = []
    for me in range(n):
        a, b = divmod(me, nb)

        def key(s):
            da, db = abs(s // nb - a), abs(s % nb - b)
            late = nb == 2 and db > 0 and s // nb == detour(a, na)
            return (da + 1.2 * db + (10 if late else 0), s)

        table.append(sorted(range(n), key=key))
    return table


def pick(me, values):
    out = jnp.int32(values[0])
    for i, v in enumerate(values[1:], 1):
        out = jnp.where(me == i, jnp.int32(v), out)
    return out


def scores_kernel(
    n, nc, target, emb, cent, shares, mass, e_x, e_v, gath, w, sq, pr, rexp,
    col_out, col_in, row_out, row_in, loc_sem, snd, rcv, csnd, crcv, rsnd, rrcv,
    esnd, ercv, fsnd, frcv, dsnd,
):
    me = lax.axis_index("dp")
    mc = lax.axis_index("cent")
    na = min(LINE, n)
    nb = n // na
    a, b = me // nb, me % nb
    rows = e_v.shape[0]
    local_k, feats = cent.shape
    piece = local_k // PIECES
    tile = min(256, piece)
    lanes = local_k // 128

    barrier = pltpu.get_barrier_semaphore()
    for k in range(1, n):
        pl.semaphore_signal(barrier, inc=1, device_id={"dp": lax.rem(me + k, n)}, device_id_type=MESH)
    for k in range(1, nc):
        pl.semaphore_signal(barrier, inc=1, device_id={"cent": lax.rem(mc + k, nc)}, device_id_type=MESH)
    pl.semaphore_wait(barrier, n - 1 + nc - 1)

    order = arrival_order(n, na, nb)

    def sends(e, src, h):
        sa, sb = src // nb, src % nb
        da, db = sa - a, sb - b
        at = pl.ds(pl.multiple_of(h * piece, piece), piece)
        ref = (cent if e == 0 else gath.at[src]).at[at]
        dst = gath.at[src].at[at]
        across = jnp.bool_(True)
        if nb == 2:
            across = jnp.logical_not((h < DETOUR) & (sa == detour(a, na)))
        conds = (
            ((db == 0) & (da <= 0) & (a < na - 1), me + nb),
            ((db == 0) & (da >= 0) & (a > 0), me - nb),
            ((db <= 0) & (b < nb - 1) & across, me + 1),
            ((db >= 0) & (b > 0) & across, me - 1),
        )
        out = []
        for i, (cond, to) in enumerate(conds):
            out.append((cond, pltpu.make_async_remote_copy(
                src_ref=ref, dst_ref=dst, send_sem=snd.at[e, i, h], recv_sem=rcv.at[src, h],
                device_id={"dp": to}, device_id_type=MESH)))
        return out

    def detour_sends(h):
        src = a * nb + 1 - b
        at = pl.ds(pl.multiple_of(h * piece, piece), piece)
        conds = (
            ((a < na - 1) & (detour(a + 1, na) == a), me + nb),
            ((a > 0) & (detour(a - 1, na) == a), me - nb),
        )
        return [(cond, pltpu.make_async_remote_copy(
            src_ref=gath.at[src].at[at], dst_ref=gath.at[src].at[at], send_sem=dsnd.at[i, h], recv_sem=rcv.at[src, h],
            device_id={"dp": to}, device_id_type=MESH)) for i, (cond, to) in enumerate(conds)]

    for h in range(PIECES):
        for cond, copy in sends(0, me, h):
            @pl.when(cond)
            def _():
                copy.start()
    part_rows = rows // nc
    mine = pl.ds(pl.multiple_of(mc * part_rows, part_rows), part_rows)
    e_copies, f_copies = [], []
    for k in range(1, nb):
        b2 = lax.rem(b + k, nb)
        for q in range(na):
            cols = pl.ds(pl.multiple_of((q * nb + b2) * feats, feats), feats)
            c = pltpu.make_async_remote_copy(
                src_ref=emb.at[mine, cols], dst_ref=e_x.at[k - 1, mine, pl.ds(q * feats, feats)],
                send_sem=esnd.at[k, q], recv_sem=ercv.at[k, q],
                device_id={"dp": a * nb + b2}, device_id_type=MESH)
            c.start()
            e_copies.append(c)
        for m in range(1, nc):
            f_copies.append(pltpu.make_async_remote_copy(
                src_ref=e_x.at[k - 1, mine], dst_ref=e_x.at[k - 1, mine],
                send_sem=fsnd.at[k, m], recv_sem=frcv.at[k, m],
                device_id={"cent": lax.rem(mc + m, nc)}, device_id_type=MESH))

    e_copy = pltpu.make_async_copy(emb, e_v, loc_sem.at[0])
    e_copy.start()
    own = pltpu.make_async_copy(cent, gath.at[me], loc_sem.at[1])
    own.start()
    e_copy.wait()

    chunk = 16

    @pl.loop(0, rows // chunk)
    def _(i):
        at = pl.ds(pl.multiple_of(i * chunk, chunk), chunk)
        x = e_v[at, :].astype(F32)
        s = jnp.sum(x * x, axis=1, keepdims=True)
        e_v[at, :] = (x * lax.rsqrt(s + 1e-06)).astype(BF16)

    own.wait()
    sq[...] = jnp.zeros_like(sq)
    ones = jnp.ones((8, feats), BF16)
    nt = (((1,), (1,)), ((), ()))

    for e in range(n):
        src = me if e == 0 else pick(me, [order[d][e] for d in range(n)])
        fcols = pl.ds(pl.multiple_of(src * feats, feats), feats)

        @pl.loop(0, PIECES)
        def _(h):
            if e > 0:
                outs = sends(e, src, h)
                outs[0][1].wait_recv()
                for cond, copy in outs:
                    @pl.when(cond)
                    def _():
                        copy.start()

            @pl.loop(0, piece // tile)
            def _(t):
                k0 = pl.multiple_of(h * piece + t * tile, tile)
                block = gath[src, pl.ds(k0, tile), :]
                part = lax.dot_general(e_v[:, fcols], block, nt, preferred_element_type=F32)
                if e == 0:
                    w[:, pl.ds(k0, tile)] = part
                else:
                    w[:, pl.ds(k0, tile)] += part
                bf = block.astype(F32)
                b2 = bf * bf
                hi = b2.astype(BF16)
                lo = (b2 - hi.astype(F32)).astype(BF16)
                sq[:, pl.ds(k0, tile)] += lax.dot_general(
                    ones, hi, nt, preferred_element_type=F32
                ) + lax.dot_general(ones, lo, nt, preferred_element_type=F32)

        if e == n // 2 - 1:
            for c in e_copies:
                c.wait()
            for c in f_copies:
                c.start()
        if nb == 2 and e == n // 2 + 1:
            for h in range(DETOUR):
                for cond, copy in detour_sends(h):
                    @pl.when(cond)
                    def _():
                        copy.start()

    def exchange_cols(r, part8):
        col_out[r] = jnp.sum(part8, axis=0, keepdims=True)
        copies = []
        for k in range(1, n):
            c = pltpu.make_async_remote_copy(
                src_ref=col_out.at[r], dst_ref=col_in.at[r, k], send_sem=csnd.at[r, k], recv_sem=crcv.at[r, k],
                device_id={"dp": lax.rem(me + k, n)}, device_id_type=MESH)
            c.start()
            copies.append(c)
        total = col_out[r]
        for k, c in enumerate(copies, 1):
            c.wait()
            total = total + col_in[r, k]
        return total

    def exchange_rows(r):
        for k in range(rows // 128):
            block = pr[k * 128:(k + 1) * 128, :]
            row_out[r, k:k + 1, :] = jnp.sum(block.T, axis=0, keepdims=True)
        copies = []
        for k in range(1, nc):
            c = pltpu.make_async_remote_copy(
                src_ref=row_out.at[r], dst_ref=row_in.at[r, k], send_sem=rsnd.at[r, k], recv_sem=rrcv.at[r, k],
                device_id={"cent": lax.rem(mc + k, nc)}, device_id_type=MESH)
            c.start()
            copies.append(c)
        total = row_out[r]
        for k, c in enumerate(copies, 1):
            c.wait()
            total = total + row_in[r, k]
        inv = 1.0 / total
        for k in range(rows // 128):
            rexp[k * 128:(k + 1) * 128, :] = jnp.broadcast_to(inv[k:k + 1, :], (128, 128)).T

    def wide(x):
        return jnp.concatenate([x] * lanes, axis=1)

    def narrow(x):
        out = x[:, :128]
        for t in range(1, lanes):
            out = out + x[:, t * 128:(t + 1) * 128]
        return out

    scale8 = lax.rsqrt(sq[...] + 1e-06) * 20.0
    zero8 = jnp.zeros((8, local_k), F32)

    def exp_pass(i, acc):
        at = pl.ds(pl.multiple_of(i * 8, 8), 8)
        x = jnp.exp(w[at, :] * scale8)
        w[at, :] = x
        return acc + x

    part8 = lax.fori_loop(0, rows // 8, exp_pass, zero8)
    for r in range(ROUNDS):
        if r > 0:
            def col_pass(i, acc):
                at = pl.ds(pl.multiple_of(i * 8, 8), 8)
                return acc + w[at, :] * wide(rexp[at, :])

            part8 = lax.fori_loop(0, rows // 8, col_pass, zero8)
        c8 = jnp.broadcast_to(target / exchange_cols(r, part8), (8, local_k))

        def row_pass(i, _):
            at = pl.ds(pl.multiple_of(i * 8, 8), 8)
            pr[at, :] = narrow(w[at, :] * c8)
            return 0

        lax.fori_loop(0, rows // 8, row_pass, 0)
        exchange_rows(r)

    c16 = jnp.broadcast_to(c8[:1], (16, local_k))

    def share_pass(i, acc):
        at = pl.ds(pl.multiple_of(i * 16, 16), 16)
        s = (w[at, :] * wide(rexp[at, :]) * c16).astype(BF16)
        shares[at, :] = s
        s = s.astype(F32)
        return acc + (s[:8] + s[8:])

    part8 = lax.fori_loop(0, rows // 16, share_pass, zero8)
    mass[...] = exchange_cols(ROUNDS, part8)
    for c in f_copies:
        c.wait()

    for e in range(n):
        src = me if e == 0 else pick(me, [order[d][e] for d in range(n)])
        for h in range(PIECES):
            for cond, copy in sends(e, src, h):
                @pl.when(cond)
                def _():
                    copy.wait_send()
    if nb == 2:
        for h in range(DETOUR):
            for cond, copy in detour_sends(h):
                @pl.when(cond)
                def _():
                    copy.wait_send()


def balanced(n, nc, embeddings, centroids):
    rows, width = embeddings.shape
    local_k, feats = centroids.shape
    target = rows * n / (local_k * nc)
    na = min(LINE, n)
    nb = n // na
    vmem = pl.BlockSpec(memory_space=pltpu.VMEM)
    dma = pltpu.SemaphoreType.DMA
    return pl.pallas_call(
        functools.partial(scores_kernel, n, nc, target),
        out_shape=(
            jax.ShapeDtypeStruct((rows, local_k), BF16),
            jax.ShapeDtypeStruct((1, local_k), F32),
            jax.ShapeDtypeStruct((nb - 1, rows, na * feats), BF16),
        ),
        in_specs=[pl.BlockSpec(memory_space=pl.ANY)] * 2,
        out_specs=(vmem, vmem, pl.BlockSpec(memory_space=pl.ANY)),
        scratch_shapes=[
            pltpu.VMEM((rows, width), BF16),
            pltpu.VMEM((n, local_k, feats), BF16),
            pltpu.VMEM((rows, local_k), F32),
            pltpu.VMEM((8, local_k), F32),
            pltpu.VMEM((rows, 128), F32),
            pltpu.VMEM((rows, 128), F32),
            pltpu.VMEM((ROUNDS + 1, 1, local_k), F32),
            pltpu.VMEM((ROUNDS + 1, n, 1, local_k), F32),
            pltpu.VMEM((ROUNDS, rows // 128, 128), F32),
            pltpu.VMEM((ROUNDS, nc, rows // 128, 128), F32),
            dma((2,)),
            dma((n, 4, PIECES)),
            dma((n, PIECES)),
            dma((ROUNDS + 1, n)),
            dma((ROUNDS + 1, n)),
            dma((ROUNDS, nc)),
            dma((ROUNDS, nc)),
            dma((nb, na)),
            dma((nb, na)),
            dma((nb, nc)),
            dma((nb, nc)),
            dma((2, PIECES)),
        ],
        compiler_params=pltpu.CompilerParams(
            collective_id=0, has_side_effects=True, vmem_limit_bytes=58 * 2**20
        ),
        cost_estimate=pl.CostEstimate(
            flops=2 * rows * width * local_k, bytes_accessed=48 * 2**20, transcendentals=rows * local_k
        ),
    )(embeddings, centroids)


def means_kernel(
    n, chunk, emb, shares, mass, e_x, out, s_v, s_x, e_v, ex_v, st, slots, p_own, p_now,
    loc_sem, xsnd, xrcv, snd, rcv,
):
    me = lax.axis_index("dp")
    na = min(LINE, n)
    nb = n // na
    a, b = me // nb, me % nb
    rows, local_k = s_v.shape
    feats = out.shape[1]
    chunks = local_k // chunk

    barrier = pltpu.get_barrier_semaphore()
    for k in range(1, nb):
        pl.semaphore_signal(
            barrier, inc=1, device_id={"dp": a * nb + lax.rem(b + k, nb)}, device_id_type=MESH)

    @pl.when(a > 0)
    def _():
        pl.semaphore_signal(barrier, inc=1, device_id={"dp": me - nb}, device_id_type=MESH)

    @pl.when(a < na - 1)
    def _():
        pl.semaphore_signal(barrier, inc=1, device_id={"dp": me + nb}, device_id_type=MESH)

    neighbours = jnp.where(a > 0, 1, 0) + jnp.where(a < na - 1, 1, 0) + nb - 1
    pl.semaphore_wait(barrier, neighbours)

    def span(j):
        return pl.ds(pl.multiple_of(j * chunk, chunk), chunk)

    def share_copy(j, k):
        return pltpu.make_async_remote_copy(
            src_ref=shares.at[:, span(j)], dst_ref=s_x.at[k - 1, :, span(j)],
            send_sem=xsnd.at[j, k], recv_sem=xrcv.at[j, k],
            device_id={"dp": a * nb + lax.rem(b + k, nb)}, device_id_type=MESH)

    @pl.loop(0, chunks)
    def _(j):
        for k in range(1, nb):
            share_copy(j, k).start()

    loads = [pltpu.make_async_copy(shares, s_v, loc_sem.at[0]), pltpu.make_async_copy(e_x, ex_v, loc_sem.at[1])]
    for q in range(na):
        cols = pl.ds(pl.multiple_of((q * nb + b) * feats, feats), feats)
        loads.append(pltpu.make_async_copy(
            emb.at[:, cols], e_v.at[:, pl.ds(q * feats, feats)], loc_sem.at[2 + q]))
    for c in loads:
        c.start()
    for c in loads:
        c.wait()

    far_first = [sorted(range(na), key=lambda q: (-abs(q - m), q)) for m in range(na)]

    def up_copy(j, q):
        return pltpu.make_async_remote_copy(
            src_ref=slots.at[j, q], dst_ref=slots.at[j, q], send_sem=snd.at[j, q], recv_sem=rcv.at[j, q],
            device_id={"dp": me + nb}, device_id_type=MESH)

    def down_copy(j, q):
        to = jnp.where(q == a - 1, na, q)
        return pltpu.make_async_remote_copy(
            src_ref=slots.at[j, q], dst_ref=slots.at[j, to], send_sem=snd.at[j, q], recv_sem=rcv.at[j, to],
            device_id={"dp": me - nb}, device_id_type=MESH)

    def arrived(j, q):
        pltpu.make_async_remote_copy(
            src_ref=slots.at[j, q], dst_ref=slots.at[j, q], send_sem=snd.at[j, 0], recv_sem=rcv.at[j, q],
            device_id={"dp": me}, device_id_type=MESH).wait_recv()

    def send_chunk(j):
        for k in range(1, nb):
            share_copy(j, k).wait_recv()
        st[0] = s_v[:, span(j)].T
        for k in range(1, nb):
            st[k] = s_x[k - 1, :, span(j)].T
        for i in range(na):
            q = pick(a, [far_first[m][i] for m in range(na)])
            cols = pl.ds(pl.multiple_of(q * feats, feats), feats)
            p = jnp.dot(st[0], e_v[:, cols], preferred_element_type=F32)
            for k in range(1, nb):
                p = p + jnp.dot(st[k], ex_v[k - 1, :, cols], preferred_element_type=F32)
            if i == na - 1:
                p_own[j] = p
                continue
            p_now[...] = p
            up = q > a
            has_in = (up & (a > 0)) | ((q < a) & (a < na - 1))

            @pl.when(has_in)
            def _():
                arrived(j, q)
                p_now[...] += slots[j, q].astype(F32)

            slots[j, q] = p_now[...].astype(BF16)

            @pl.when(up)
            def _():
                up_copy(j, q).start()

            @pl.when(q < a)
            def _():
                down_copy(j, q).start()

    def finish_chunk(j):
        @pl.when(a > 0)
        def _():
            arrived(j, a)
            p_own[j] += slots[j, a].astype(F32)

        @pl.when(a < na - 1)
        def _():
            arrived(j, na)
            p_own[j] += slots[j, na].astype(F32)

        for t in range(chunk // 128):
            at = pl.ds(pl.multiple_of(j * chunk + t * 128, 128), 128)
            m = jnp.broadcast_to(mass[:, at], (128, 128)).T
            m = jnp.concatenate([m] * (feats // 128), axis=1)
            out[at, :] = (p_own[j, t * 128:(t + 1) * 128, :] / m).astype(BF16)

    late = min(2, chunks)

    @pl.loop(0, chunks)
    def _(j):
        send_chunk(j)

        @pl.when(j >= late)
        def _():
            finish_chunk(j - late)

    @pl.loop(chunks - late, chunks)
    def _(j):
        finish_chunk(j)

    @pl.loop(0, chunks)
    def _(j):
        for k in range(1, nb):
            share_copy(j, k).wait_send()
        for q in range(na):
            @pl.when(a < q)
            def _():
                up_copy(j, q).wait_send()

            @pl.when(a > q)
            def _():
                down_copy(j, q).wait_send()


def means(n, embeddings, shares, mass, e_x, feats):
    rows, local_k = shares.shape
    na = min(LINE, n)
    nb = n // na
    chunk = min(256, local_k)
    chunks = local_k // chunk
    vmem = pl.BlockSpec(memory_space=pltpu.VMEM)
    hbm = pl.BlockSpec(memory_space=pl.ANY)
    dma = pltpu.SemaphoreType.DMA
    return pl.pallas_call(
        functools.partial(means_kernel, n, chunk),
        out_shape=jax.ShapeDtypeStruct((local_k, feats), BF16),
        in_specs=[hbm, hbm, vmem, hbm],
        out_specs=vmem,
        scratch_shapes=[
            pltpu.VMEM((rows, local_k), BF16),
            pltpu.VMEM((nb - 1, rows, local_k), BF16),
            pltpu.VMEM((rows, na * feats), BF16),
            pltpu.VMEM((nb - 1, rows, na * feats), BF16),
            pltpu.VMEM((nb, chunk, rows), BF16),
            pltpu.VMEM((chunks, na + 1, chunk, feats), BF16),
            pltpu.VMEM((chunks, chunk, feats), F32),
            pltpu.VMEM((chunk, feats), F32),
            dma((2 + na,)),
            dma((chunks, nb)),
            dma((chunks, nb)),
            dma((chunks, na)),
            dma((chunks, na + 1)),
        ],
        compiler_params=pltpu.CompilerParams(
            collective_id=1, has_side_effects=True, vmem_limit_bytes=58 * 2**20
        ),
        cost_estimate=pl.CostEstimate(
            flops=2 * rows * n * feats * local_k, bytes_accessed=24 * 2**20, transcendentals=0
        ),
    )(embeddings, shares, mass, e_x)


def on_device(n, nc, embeddings, centroids):
    shares, mass, e_x = balanced(n, nc, embeddings, centroids)
    new_centroids = means(n, embeddings, shares, mass, e_x, centroids.shape[1])
    return (shares, new_centroids)


def solution(mesh):
    in_specs = (P("dp", None), P("cent", "dp"))
    out_specs = (P("dp", "cent"), P("cent", "dp"))
    return jax.shard_map(
        functools.partial(on_device, mesh.shape["dp"], mesh.shape["cent"]),
        mesh=mesh, in_specs=in_specs, out_specs=out_specs, check_vma=False,
    )
```

```python
import functools

import jax
import jax.numpy as jnp
from jax import lax
from jax.experimental import pallas as pl
from jax.experimental.pallas import tpu as pltpu
from jax.sharding import PartitionSpec as P

ROUNDS = 3
LINE = 4
PIECES = 4
CHUNK = 256
DETOUR = 3
MESH = pl.DeviceIdType.MESH
F32 = jnp.float32
BF16 = jnp.bfloat16


def detour(a, na):
    if isinstance(a, int):
        return a + 1 if a < na // 2 else a - 1
    return jnp.where(a < na // 2, a + 1, a - 1)


def arrival_order(n, na, nb):
    table = []
    for me in range(n):
        a, b = divmod(me, nb)

        def key(s):
            da, db = abs(s // nb - a), abs(s % nb - b)
            late = nb == 2 and db > 0 and s // nb == detour(a, na)
            return (da + 1.2 * db + (10 if late else 0), s)

        table.append(sorted(range(n), key=key))
    return table


def pick(me, values):
    out = jnp.int32(values[0])
    for i, v in enumerate(values[1:], 1):
        out = jnp.where(me == i, jnp.int32(v), out)
    return out


def step_kernel(
    n, nc, target, chunk, emb, cent, shares, out, e_v, gath, w, sq, pr, rexp,
    s_v, s_x, e_x, st, p_own, p_now, mass, col_now, col_out, col_in, row_out, row_in, loc_sem, snd, rcv, csnd, crcv, rsnd, rrcv,
    esnd, ercv, fsnd, frcv, dsnd, xsnd, xrcv, snd2, rcv2,
):
    me = lax.axis_index("dp")
    mc = lax.axis_index("cent")
    na = min(LINE, n)
    nb = n // na
    a, b = me // nb, me % nb
    rows = e_v.shape[0]
    local_k, feats = cent.shape
    piece = local_k // PIECES
    tile = min(256, piece)
    lanes = local_k // 128

    barrier = pltpu.get_barrier_semaphore()
    for k in range(1, n):
        pl.semaphore_signal(barrier, inc=1, device_id={"dp": lax.rem(me + k, n)}, device_id_type=MESH)
    for k in range(1, nc):
        pl.semaphore_signal(barrier, inc=1, device_id={"cent": lax.rem(mc + k, nc)}, device_id_type=MESH)
    pl.semaphore_wait(barrier, n - 1 + nc - 1)

    order = arrival_order(n, na, nb)

    def sends(e, src, h):
        sa, sb = src // nb, src % nb
        da, db = sa - a, sb - b
        dst = gath.at[pl.ds(pl.multiple_of(src * local_k + h * piece, piece), piece)]
        ref = cent.at[pl.ds(pl.multiple_of(h * piece, piece), piece)] if e == 0 else dst
        across = jnp.bool_(True)
        if nb == 2:
            across = jnp.logical_not((h < DETOUR) & (sa == detour(a, na)))
        conds = (
            ((db == 0) & (da <= 0) & (a < na - 1), me + nb),
            ((db == 0) & (da >= 0) & (a > 0), me - nb),
            ((db <= 0) & (b < nb - 1) & across, me + 1),
            ((db >= 0) & (b > 0) & across, me - 1),
        )
        out = []
        for i, (cond, to) in enumerate(conds):
            out.append((cond, pltpu.make_async_remote_copy(
                src_ref=ref, dst_ref=dst, send_sem=snd.at[e, i, h], recv_sem=rcv.at[src, h],
                device_id={"dp": to}, device_id_type=MESH)))
        return out

    def detour_sends(h):
        src = a * nb + 1 - b
        ref = gath.at[pl.ds(pl.multiple_of(src * local_k + h * piece, piece), piece)]
        conds = (
            ((a < na - 1) & (detour(a + 1, na) == a), me + nb),
            ((a > 0) & (detour(a - 1, na) == a), me - nb),
        )
        return [(cond, pltpu.make_async_remote_copy(
            src_ref=ref, dst_ref=ref, send_sem=dsnd.at[i, h], recv_sem=rcv.at[src, h],
            device_id={"dp": to}, device_id_type=MESH)) for i, (cond, to) in enumerate(conds)]

    for h in range(PIECES):
        for cond, copy in sends(0, me, h):
            @pl.when(cond)
            def _():
                copy.start()
    part_rows = rows // nc
    mine = pl.ds(pl.multiple_of(mc * part_rows, part_rows), part_rows)
    e_copies, f_copies = [], []
    for k in range(1, nb):
        b2 = lax.rem(b + k, nb)
        for q in range(na):
            cols = pl.ds(pl.multiple_of((q * nb + b2) * feats, feats), feats)
            c = pltpu.make_async_remote_copy(
                src_ref=emb.at[mine, cols], dst_ref=e_x.at[k - 1, mine, pl.ds(q * feats, feats)],
                send_sem=esnd.at[k, q], recv_sem=ercv.at[k, q],
                device_id={"dp": a * nb + b2}, device_id_type=MESH)
            c.start()
            e_copies.append(c)
        for m in range(1, nc):
            f_copies.append(pltpu.make_async_remote_copy(
                src_ref=e_x.at[k - 1, mine], dst_ref=e_x.at[k - 1, mine],
                send_sem=fsnd.at[k, m], recv_sem=frcv.at[k, m],
                device_id={"cent": lax.rem(mc + m, nc)}, device_id_type=MESH))

    e_copy = pltpu.make_async_copy(emb, e_v, loc_sem.at[0])
    e_copy.start()
    own = pltpu.make_async_copy(
        cent, gath.at[pl.ds(pl.multiple_of(me * local_k, local_k), local_k)], loc_sem.at[1])
    own.start()
    e_copy.wait()

    @pl.loop(0, rows // 16)
    def _(i):
        at = pl.ds(pl.multiple_of(i * 16, 16), 16)
        x = e_v[at, :].astype(F32)
        s = jnp.sum(x * x, axis=1, keepdims=True)
        e_v[at, :] = (x * lax.rsqrt(s + 1e-06)).astype(BF16)

    own.wait()
    sq[...] = jnp.zeros_like(sq)
    ones = jnp.ones((8, feats), BF16)
    nt = (((1,), (1,)), ((), ()))

    for e in range(n):
        src = me if e == 0 else pick(me, [order[d][e] for d in range(n)])
        fcols = pl.ds(pl.multiple_of(src * feats, feats), feats)

        @pl.loop(0, PIECES)
        def _(h):
            if e > 0:
                outs = sends(e, src, h)
                outs[0][1].wait_recv()
                for cond, copy in outs:
                    @pl.when(cond)
                    def _():
                        copy.start()

            @pl.loop(0, piece // tile)
            def _(t):
                k0 = pl.multiple_of(h * piece + t * tile, tile)
                block = gath[pl.ds(pl.multiple_of(src * local_k + k0, tile), tile), :]
                part = lax.dot_general(e_v[:, fcols], block, nt, preferred_element_type=F32)
                if e == 0:
                    w[:, pl.ds(k0, tile)] = part
                else:
                    w[:, pl.ds(k0, tile)] += part
                bf = block.astype(F32)
                b2 = bf * bf
                hi = b2.astype(BF16)
                lo = (b2 - hi.astype(F32)).astype(BF16)
                sq[:, pl.ds(k0, tile)] += lax.dot_general(
                    ones, hi, nt, preferred_element_type=F32
                ) + lax.dot_general(ones, lo, nt, preferred_element_type=F32)

        if e == n // 2 - 1:
            for c in e_copies:
                c.wait()
            for c in f_copies:
                c.start()
        if nb == 2 and e == n // 2 + 1:
            for h in range(DETOUR):
                for cond, copy in detour_sends(h):
                    @pl.when(cond)
                    def _():
                        copy.start()

    for e in range(n):
        src = me if e == 0 else pick(me, [order[d][e] for d in range(n)])
        for h in range(PIECES):
            for cond, copy in sends(e, src, h):
                @pl.when(cond)
                def _():
                    copy.wait_send()
    if nb == 2:
        for h in range(DETOUR):
            for cond, copy in detour_sends(h):
                @pl.when(cond)
                def _():
                    copy.wait_send()

    for c in f_copies:
        c.wait()
    e_copy.start()

    def col_copies(r):
        return [pltpu.make_async_remote_copy(
            src_ref=col_out.at[r], dst_ref=col_in.at[r, k], send_sem=csnd.at[r, k], recv_sem=crcv.at[r, k],
            device_id={"dp": lax.rem(me + k, n)}, device_id_type=MESH) for k in range(1, n)]

    def exchange_cols(r, part8):
        col_out[r] = jnp.sum(part8, axis=0, keepdims=True)
        copies = col_copies(r)
        for c in copies:
            c.start()
        total = col_out[r]
        for k, c in enumerate(copies, 1):
            c.wait()
            total = total + col_in[r, k]
        return total

    def exchange_rows(r):
        for k in range(rows // 128):
            block = pr[k * 128:(k + 1) * 128, :]
            row_out[r, k:k + 1, :] = jnp.sum(block.T, axis=0, keepdims=True)
        copies = []
        for k in range(1, nc):
            c = pltpu.make_async_remote_copy(
                src_ref=row_out.at[r], dst_ref=row_in.at[r, k], send_sem=rsnd.at[r, k], recv_sem=rrcv.at[r, k],
                device_id={"cent": lax.rem(mc + k, nc)}, device_id_type=MESH)
            c.start()
            copies.append(c)
        total = row_out[r]
        for k, c in enumerate(copies, 1):
            c.wait()
            total = total + row_in[r, k]
        inv = 1.0 / total
        for k in range(rows // 128):
            rexp[k * 128:(k + 1) * 128, :] = jnp.broadcast_to(inv[k:k + 1, :], (128, 128)).T

    def wide(x):
        return jnp.concatenate([x] * lanes, axis=1)

    def narrow(x):
        parts = [x[:, t * 128:(t + 1) * 128] for t in range(lanes)]
        while len(parts) > 1:
            half = [p + q for p, q in zip(parts[::2], parts[1::2])]
            parts = half + parts[len(half) * 2:]
        return parts[0]

    scale8 = lax.rsqrt(sq[...] + 1e-06) * 20.0
    zero8 = jnp.zeros((8, local_k), F32)

    def exp_pass(i, acc):
        at = pl.ds(pl.multiple_of(i * 8, 8), 8)
        x = jnp.exp(w[at, :] * scale8)
        w[at, :] = x
        return acc + x

    part8 = lax.fori_loop(0, rows // 8, exp_pass, zero8, unroll=4)
    for r in range(ROUNDS):
        if r > 0:
            def col_pass(i, acc):
                at = pl.ds(pl.multiple_of(i * 8, 8), 8)
                return acc + w[at, :] * wide(rexp[at, :])

            part8 = lax.fori_loop(0, rows // 8, col_pass, zero8, unroll=4)
        c8 = jnp.broadcast_to(target / exchange_cols(r, part8), (8, local_k))

        def row_pass(i, _):
            at = pl.ds(pl.multiple_of(i * 8, 8), 8)
            pr[at, :] = narrow(w[at, :] * c8)
            return 0

        lax.fori_loop(0, rows // 8, row_pass, 0, unroll=4)
        exchange_rows(r)

    chunks = local_k // chunk

    def span(j):
        return pl.ds(pl.multiple_of(j * chunk, chunk), chunk)

    def share_copy(j, k):
        return pltpu.make_async_remote_copy(
            src_ref=s_v.at[:, span(j)], dst_ref=s_x.at[k - 1, :, span(j)],
            send_sem=xsnd.at[j, k], recv_sem=xrcv.at[j, k],
            device_id={"dp": a * nb + lax.rem(b + k, nb)}, device_id_type=MESH)

    col_now[...] = c8[:1]
    last = ROUNDS

    @pl.loop(0, chunks)
    def _(j):
        c16 = jnp.broadcast_to(col_now[:, span(j)], (16, chunk))

        def share_pass(i, acc):
            at = pl.ds(pl.multiple_of(i * 16, 16), 16)
            r = rexp[at, :]
            x = (w[at, span(j)] * jnp.concatenate([r] * (chunk // 128), axis=1) * c16).astype(BF16)
            s_v[at, span(j)] = x
            x = x.astype(F32)
            return acc + (x[:8] + x[8:])

        part = lax.fori_loop(0, rows // 16, share_pass, jnp.zeros((8, chunk), F32), unroll=4)
        col_out[last, :, span(j)] = jnp.sum(part, axis=0, keepdims=True)
        for k in range(1, nb):
            share_copy(j, k).start()

    mass_copies = col_copies(last)
    for c in mass_copies:
        c.start()
    s_copy = pltpu.make_async_copy(s_v, shares, loc_sem.at[1])
    s_copy.start()
    e_copy.wait()

    def slot_at(j, q):
        return pl.ds(pl.multiple_of((j * (na + 1) + q) * chunk, chunk), chunk)

    def slot(j, q):
        return gath.at[slot_at(j, q)]

    far_first = [sorted(range(na), key=lambda q: (-abs(q - m), q)) for m in range(na)]

    def up_copy(j, q):
        return pltpu.make_async_remote_copy(
            src_ref=slot(j, q), dst_ref=slot(j, q), send_sem=snd2.at[j, q], recv_sem=rcv2.at[j, q],
            device_id={"dp": me + nb}, device_id_type=MESH)

    def down_copy(j, q):
        to = jnp.where(q == a - 1, na, q)
        return pltpu.make_async_remote_copy(
            src_ref=slot(j, q), dst_ref=slot(j, to), send_sem=snd2.at[j, q], recv_sem=rcv2.at[j, to],
            device_id={"dp": me - nb}, device_id_type=MESH)

    def arrived(j, q):
        pltpu.make_async_remote_copy(
            src_ref=slot(j, q), dst_ref=slot(j, q), send_sem=snd2.at[j, 0], recv_sem=rcv2.at[j, q],
            device_id={"dp": me}, device_id_type=MESH).wait_recv()

    def send_chunk(j):
        for k in range(1, nb):
            share_copy(j, k).wait_recv()
        st[0] = s_v[:, span(j)].T
        for k in range(1, nb):
            st[k] = s_x[k - 1, :, span(j)].T
        for i in range(na):
            q = pick(a, [far_first[m][i] for m in range(na)])
            cols = pl.ds(pl.multiple_of(q * feats, feats), feats)
            own_cols = pl.ds(pl.multiple_of((q * nb + b) * feats, feats), feats)
            p = jnp.dot(st[0], e_v[:, own_cols], preferred_element_type=F32)
            for k in range(1, nb):
                p = p + jnp.dot(st[k], e_x[k - 1, :, cols], preferred_element_type=F32)
            if i == na - 1:
                p_own[j] = p
                continue
            p_now[...] = p
            up = q > a
            has_in = (up & (a > 0)) | ((q < a) & (a < na - 1))

            @pl.when(has_in)
            def _():
                arrived(j, q)
                p_now[...] += gath[slot_at(j, q), :].astype(F32)

            gath[slot_at(j, q), :] = p_now[...].astype(BF16)

            @pl.when(up)
            def _():
                up_copy(j, q).start()

            @pl.when(q < a)
            def _():
                down_copy(j, q).start()

    def finish_chunk(j):
        @pl.when(a > 0)
        def _():
            arrived(j, a)
            p_own[j] += gath[slot_at(j, a), :].astype(F32)

        @pl.when(a < na - 1)
        def _():
            arrived(j, na)
            p_own[j] += gath[slot_at(j, na), :].astype(F32)

        for t in range(chunk // 128):
            at = pl.ds(pl.multiple_of(j * chunk + t * 128, 128), 128)
            m = jnp.broadcast_to(mass[:, at], (128, 128)).T
            m = jnp.concatenate([m] * (feats // 128), axis=1)
            out[at, :] = (p_own[j, t * 128:(t + 1) * 128, :] / m).astype(BF16)

    late = min(2, chunks - 1)

    @pl.loop(0, chunks)
    def _(j):
        send_chunk(j)

        @pl.when(j == late)
        def _():
            total = col_out[last]
            for k, c in enumerate(mass_copies, 1):
                c.wait()
                total = total + col_in[last, k]
            mass[...] = total

        @pl.when(j >= late)
        def _():
            finish_chunk(j - late)

    @pl.loop(chunks - late, chunks)
    def _(j):
        finish_chunk(j)

    @pl.loop(0, chunks)
    def _(j):
        for k in range(1, nb):
            share_copy(j, k).wait_send()
        for q in range(na):
            @pl.when(a < q)
            def _():
                up_copy(j, q).wait_send()

            @pl.when(a > q)
            def _():
                down_copy(j, q).wait_send()
    s_copy.wait()


def on_device(n, nc, embeddings, centroids):
    rows, width = embeddings.shape
    local_k, feats = centroids.shape
    target = rows * n / (local_k * nc)
    na = min(LINE, n)
    nb = n // na
    chunk = min(CHUNK, local_k)
    chunks = local_k // chunk
    vmem = pltpu.VMEM
    dma = pltpu.SemaphoreType.DMA
    hbm = pl.BlockSpec(memory_space=pl.ANY)
    return pl.pallas_call(
        functools.partial(step_kernel, n, nc, target, chunk),
        out_shape=(
            jax.ShapeDtypeStruct((rows, local_k), BF16),
            jax.ShapeDtypeStruct((local_k, feats), BF16),
        ),
        in_specs=[hbm, hbm],
        out_specs=(hbm, pl.BlockSpec(memory_space=pltpu.VMEM)),
        scratch_shapes=[
            vmem((rows, width), BF16),
            vmem((n * local_k, feats), BF16),
            vmem((rows, local_k), F32),
            vmem((8, local_k), F32),
            vmem((rows, 128), F32),
            vmem((rows, 128), F32),
            vmem((rows, local_k), BF16),
            vmem((nb - 1, rows, local_k), BF16),
            vmem((nb - 1, rows, na * feats), BF16),
            vmem((nb, chunk, rows), BF16),
            vmem((chunks, chunk, feats), F32),
            vmem((chunk, feats), F32),
            vmem((1, local_k), F32),
            vmem((1, local_k), F32),
            vmem((ROUNDS + 1, 1, local_k), F32),
            vmem((ROUNDS + 1, n, 1, local_k), F32),
            vmem((ROUNDS, rows // 128, 128), F32),
            vmem((ROUNDS, nc, rows // 128, 128), F32),
            dma((2,)),
            dma((n, 4, PIECES)),
            dma((n, PIECES)),
            dma((ROUNDS + 1, n)),
            dma((ROUNDS + 1, n)),
            dma((ROUNDS, nc)),
            dma((ROUNDS, nc)),
            dma((nb, na)),
            dma((nb, na)),
            dma((nb, nc)),
            dma((nb, nc)),
            dma((2, PIECES)),
            dma((chunks, nb)),
            dma((chunks, nb)),
            dma((chunks, na)),
            dma((chunks, na + 1)),
        ],
        compiler_params=pltpu.CompilerParams(
            collective_id=0, has_side_effects=True, vmem_limit_bytes=60 * 2**20
        ),
        cost_estimate=pl.CostEstimate(
            flops=4 * rows * width * local_k, bytes_accessed=48 * 2**20, transcendentals=rows * local_k
        ),
    )(embeddings, centroids)


def solution(mesh):
    in_specs = (P("dp", None), P("cent", "dp"))
    out_specs = (P("dp", "cent"), P("cent", "dp"))
    return jax.shard_map(
        functools.partial(on_device, mesh.shape["dp"], mesh.shape["cent"]),
        mesh=mesh, in_specs=in_specs, out_specs=out_specs, check_vma=False,
    )
```

```python
import functools

import jax
import jax.numpy as jnp
from jax import lax
from jax.experimental import pallas as pl
from jax.experimental.pallas import tpu as pltpu
from jax.sharding import PartitionSpec as P

ROUNDS = 3
LINE = 4
PIECES = 4
CHUNK = 256
DETOUR = 3
MESH = pl.DeviceIdType.MESH
F32 = jnp.float32
BF16 = jnp.bfloat16


def detour(a, na):
    if isinstance(a, int):
        return a + 1 if a < na // 2 else a - 1
    return jnp.where(a < na // 2, a + 1, a - 1)


def arrival_order(n, na, nb):
    table = []
    for me in range(n):
        a, b = divmod(me, nb)

        def key(s):
            da, db = abs(s // nb - a), abs(s % nb - b)
            late = nb == 2 and db > 0 and s // nb == detour(a, na)
            return (da + 1.2 * db + (10 if late else 0), s)

        table.append(sorted(range(n), key=key))
    return table


def pick(me, values):
    out = jnp.int32(values[0])
    for i, v in enumerate(values[1:], 1):
        out = jnp.where(me == i, jnp.int32(v), out)
    return out


def step_kernel(
    n, nc, target, chunk, emb, cent, shares, out, e_v, gath, w, sq, pr, rexp,
    s_v, s_x, e_x, st, p_own, p_now, mass, col_now, col_out, col_in, row_out, row_in, loc_sem, snd, rcv, csnd, crcv, rsnd, rrcv,
    esnd, ercv, fsnd, frcv, dsnd, xsnd, xrcv, snd2, rcv2,
):
    me = lax.axis_index("dp")
    mc = lax.axis_index("cent")
    na = min(LINE, n)
    nb = n // na
    a, b = me // nb, me % nb
    rows = e_v.shape[0]
    local_k, feats = cent.shape
    piece = local_k // PIECES
    tile = min(256, piece)
    lanes = local_k // 128

    barrier = pltpu.get_barrier_semaphore()
    for k in range(1, n):
        pl.semaphore_signal(barrier, inc=1, device_id={"dp": lax.rem(me + k, n)}, device_id_type=MESH)
    for k in range(1, nc):
        pl.semaphore_signal(barrier, inc=1, device_id={"cent": lax.rem(mc + k, nc)}, device_id_type=MESH)
    pl.semaphore_wait(barrier, n - 1 + nc - 1)

    order = arrival_order(n, na, nb)

    def sends(e, src, h):
        sa, sb = src // nb, src % nb
        da, db = sa - a, sb - b
        dst = gath.at[pl.ds(pl.multiple_of(src * local_k + h * piece, piece), piece)]
        ref = cent.at[pl.ds(pl.multiple_of(h * piece, piece), piece)] if e == 0 else dst
        across = jnp.bool_(True)
        if nb == 2:
            across = jnp.logical_not((h < DETOUR) & (sa == detour(a, na)))
        conds = (
            ((db == 0) & (da <= 0) & (a < na - 1), me + nb),
            ((db == 0) & (da >= 0) & (a > 0), me - nb),
            ((db <= 0) & (b < nb - 1) & across, me + 1),
            ((db >= 0) & (b > 0) & across, me - 1),
        )
        out = []
        for i, (cond, to) in enumerate(conds):
            out.append((cond, pltpu.make_async_remote_copy(
                src_ref=ref, dst_ref=dst, send_sem=snd.at[e, i, h], recv_sem=rcv.at[src, h],
                device_id={"dp": to}, device_id_type=MESH)))
        return out

    def detour_sends(h):
        src = a * nb + 1 - b
        ref = gath.at[pl.ds(pl.multiple_of(src * local_k + h * piece, piece), piece)]
        conds = (
            ((a < na - 1) & (detour(a + 1, na) == a), me + nb),
            ((a > 0) & (detour(a - 1, na) == a), me - nb),
        )
        return [(cond, pltpu.make_async_remote_copy(
            src_ref=ref, dst_ref=ref, send_sem=dsnd.at[i, h], recv_sem=rcv.at[src, h],
            device_id={"dp": to}, device_id_type=MESH)) for i, (cond, to) in enumerate(conds)]

    for h in range(PIECES):
        for cond, copy in sends(0, me, h):
            @pl.when(cond)
            def _():
                copy.start()
    part_rows = rows // nc
    mine = pl.ds(pl.multiple_of(mc * part_rows, part_rows), part_rows)
    e_copies, f_copies = [], []
    for k in range(1, nb):
        b2 = lax.rem(b + k, nb)
        for q in range(na):
            cols = pl.ds(pl.multiple_of((q * nb + b2) * feats, feats), feats)
            c = pltpu.make_async_remote_copy(
                src_ref=emb.at[mine, cols], dst_ref=e_x.at[k - 1, mine, pl.ds(q * feats, feats)],
                send_sem=esnd.at[k, q], recv_sem=ercv.at[k, q],
                device_id={"dp": a * nb + b2}, device_id_type=MESH)
            c.start()
            e_copies.append(c)
        for m in range(1, nc):
            f_copies.append(pltpu.make_async_remote_copy(
                src_ref=e_x.at[k - 1, mine], dst_ref=e_x.at[k - 1, mine],
                send_sem=fsnd.at[k, m], recv_sem=frcv.at[k, m],
                device_id={"cent": lax.rem(mc + m, nc)}, device_id_type=MESH))

    e_copy = pltpu.make_async_copy(emb, e_v, loc_sem.at[0])
    e_copy.start()
    own = pltpu.make_async_copy(
        cent, gath.at[pl.ds(pl.multiple_of(me * local_k, local_k), local_k)], loc_sem.at[1])
    own.start()
    e_copy.wait()

    @pl.loop(0, rows // 16)
    def _(i):
        at = pl.ds(pl.multiple_of(i * 16, 16), 16)
        x = e_v[at, :].astype(F32)
        s = jnp.sum(x * x, axis=1, keepdims=True)
        e_v[at, :] = (x * lax.rsqrt(s + 1e-06)).astype(BF16)

    own.wait()
    sq[...] = jnp.zeros_like(sq)
    ones = jnp.ones((8, feats), BF16)
    nt = (((1,), (1,)), ((), ()))

    for e in range(n):
        src = me if e == 0 else pick(me, [order[d][e] for d in range(n)])
        fcols = pl.ds(pl.multiple_of(src * feats, feats), feats)

        @pl.loop(0, PIECES)
        def _(h):
            if e > 0:
                outs = sends(e, src, h)
                outs[0][1].wait_recv()
                for cond, copy in outs:
                    @pl.when(cond)
                    def _():
                        copy.start()

            @pl.loop(0, piece // tile)
            def _(t):
                k0 = pl.multiple_of(h * piece + t * tile, tile)
                block = gath[pl.ds(pl.multiple_of(src * local_k + k0, tile), tile), :]
                part = lax.dot_general(e_v[:, fcols], block, nt, preferred_element_type=F32)
                if e == 0:
                    w[:, pl.ds(k0, tile)] = part
                else:
                    w[:, pl.ds(k0, tile)] += part
                bf = block.astype(F32)
                b2 = bf * bf
                hi = b2.astype(BF16)
                lo = (b2 - hi.astype(F32)).astype(BF16)
                sq[:, pl.ds(k0, tile)] += lax.dot_general(
                    ones, hi, nt, preferred_element_type=F32
                ) + lax.dot_general(ones, lo, nt, preferred_element_type=F32)

        if e == n // 2 - 1:
            for c in e_copies:
                c.wait()
            for c in f_copies:
                c.start()
        if nb == 2 and e == n // 2 + 1:
            for h in range(DETOUR):
                for cond, copy in detour_sends(h):
                    @pl.when(cond)
                    def _():
                        copy.start()

    for e in range(n):
        src = me if e == 0 else pick(me, [order[d][e] for d in range(n)])
        for h in range(PIECES):
            for cond, copy in sends(e, src, h):
                @pl.when(cond)
                def _():
                    copy.wait_send()
    if nb == 2:
        for h in range(DETOUR):
            for cond, copy in detour_sends(h):
                @pl.when(cond)
                def _():
                    copy.wait_send()

    for c in f_copies:
        c.wait()
    e_copy.start()

    def col_copies(r):
        return [pltpu.make_async_remote_copy(
            src_ref=col_out.at[r], dst_ref=col_in.at[r, k], send_sem=csnd.at[r, k], recv_sem=crcv.at[r, k],
            device_id={"dp": lax.rem(me + k, n)}, device_id_type=MESH) for k in range(1, n)]

    def exchange_cols(r, part8):
        col_out[r] = jnp.sum(part8, axis=0, keepdims=True)
        copies = col_copies(r)
        for c in copies:
            c.start()
        total = col_out[r]
        for k, c in enumerate(copies, 1):
            c.wait()
            total = total + col_in[r, k]
        return total

    def exchange_rows(r):
        for k in range(rows // 128):
            block = pr[k * 128:(k + 1) * 128, :]
            row_out[r, k:k + 1, :] = jnp.sum(block.T, axis=0, keepdims=True)
        copies = []
        for k in range(1, nc):
            c = pltpu.make_async_remote_copy(
                src_ref=row_out.at[r], dst_ref=row_in.at[r, k], send_sem=rsnd.at[r, k], recv_sem=rrcv.at[r, k],
                device_id={"cent": lax.rem(mc + k, nc)}, device_id_type=MESH)
            c.start()
            copies.append(c)
        total = row_out[r]
        for k, c in enumerate(copies, 1):
            c.wait()
            total = total + row_in[r, k]
        inv = 1.0 / total
        for k in range(rows // 128):
            rexp[k * 128:(k + 1) * 128, :] = jnp.broadcast_to(inv[k:k + 1, :], (128, 128)).T

    def wide(x):
        return jnp.concatenate([x] * lanes, axis=1)

    def narrow(x):
        parts = [x[:, t * 128:(t + 1) * 128] for t in range(lanes)]
        while len(parts) > 1:
            half = [p + q for p, q in zip(parts[::2], parts[1::2])]
            parts = half + parts[len(half) * 2:]
        return parts[0]

    scale8 = lax.rsqrt(sq[...] + 1e-06) * 20.0
    zero8 = jnp.zeros((8, local_k), F32)

    def exp_pass(i, acc):
        at = pl.ds(pl.multiple_of(i * 8, 8), 8)
        x = jnp.exp(w[at, :] * scale8)
        w[at, :] = x
        return acc + x

    part8 = lax.fori_loop(0, rows // 8, exp_pass, zero8, unroll=4)
    for r in range(ROUNDS):
        if r > 0:
            def col_pass(i, acc):
                at = pl.ds(pl.multiple_of(i * 8, 8), 8)
                return acc + w[at, :] * wide(rexp[at, :])

            part8 = lax.fori_loop(0, rows // 8, col_pass, zero8, unroll=4)
        c8 = jnp.broadcast_to(target / exchange_cols(r, part8), (8, local_k))

        def row_pass(i, _):
            at = pl.ds(pl.multiple_of(i * 8, 8), 8)
            pr[at, :] = narrow(w[at, :] * c8)
            return 0

        lax.fori_loop(0, rows // 8, row_pass, 0, unroll=4)
        exchange_rows(r)

    chunks = local_k // chunk

    def span(j):
        return pl.ds(pl.multiple_of(j * chunk, chunk), chunk)

    def share_copy(j, k):
        return pltpu.make_async_remote_copy(
            src_ref=s_v.at[:, span(j)], dst_ref=s_x.at[k - 1, :, span(j)],
            send_sem=xsnd.at[j, k], recv_sem=xrcv.at[j, k],
            device_id={"dp": a * nb + lax.rem(b + k, nb)}, device_id_type=MESH)

    col_now[...] = c8[:1]
    last = ROUNDS

    @pl.loop(0, chunks)
    def _(j):
        c16 = jnp.broadcast_to(col_now[:, span(j)], (16, chunk))

        def share_pass(i, acc):
            at = pl.ds(pl.multiple_of(i * 16, 16), 16)
            r = rexp[at, :]
            x = (w[at, span(j)] * jnp.concatenate([r] * (chunk // 128), axis=1) * c16).astype(BF16)
            s_v[at, span(j)] = x
            x = x.astype(F32)
            return acc + (x[:8] + x[8:])

        part = lax.fori_loop(0, rows // 16, share_pass, jnp.zeros((8, chunk), F32), unroll=4)
        col_out[last, :, span(j)] = jnp.sum(part, axis=0, keepdims=True)

        @pl.when(j == 0)
        def _():
            for k in range(1, nb):
                share_copy(j, k).start()

    mass_copies = col_copies(last)
    for c in mass_copies:
        c.start()

    @pl.loop(1, chunks)
    def _(j):
        for k in range(1, nb):
            share_copy(j, k).start()

    s_copy = pltpu.make_async_copy(s_v, shares, loc_sem.at[1])
    s_copy.start()
    e_copy.wait()

    def slot_at(j, q):
        return pl.ds(pl.multiple_of((j * (na + 1) + q) * chunk, chunk), chunk)

    def slot(j, q):
        return gath.at[slot_at(j, q)]

    far_first = [sorted(range(na), key=lambda q: (-abs(q - m), q)) for m in range(na)]

    def up_copy(j, q):
        return pltpu.make_async_remote_copy(
            src_ref=slot(j, q), dst_ref=slot(j, q), send_sem=snd2.at[j, q], recv_sem=rcv2.at[j, q],
            device_id={"dp": me + nb}, device_id_type=MESH)

    def down_copy(j, q):
        to = jnp.where(q == a - 1, na, q)
        return pltpu.make_async_remote_copy(
            src_ref=slot(j, q), dst_ref=slot(j, to), send_sem=snd2.at[j, q], recv_sem=rcv2.at[j, to],
            device_id={"dp": me - nb}, device_id_type=MESH)

    def arrived(j, q):
        pltpu.make_async_remote_copy(
            src_ref=slot(j, q), dst_ref=slot(j, q), send_sem=snd2.at[j, 0], recv_sem=rcv2.at[j, q],
            device_id={"dp": me}, device_id_type=MESH).wait_recv()

    def send_chunk(j):
        for k in range(1, nb):
            share_copy(j, k).wait_recv()
        st[0] = s_v[:, span(j)].T
        for k in range(1, nb):
            st[k] = s_x[k - 1, :, span(j)].T
        for i in range(na):
            q = pick(a, [far_first[m][i] for m in range(na)])
            cols = pl.ds(pl.multiple_of(q * feats, feats), feats)
            own_cols = pl.ds(pl.multiple_of((q * nb + b) * feats, feats), feats)
            p = jnp.dot(st[0], e_v[:, own_cols], preferred_element_type=F32)
            for k in range(1, nb):
                p = p + jnp.dot(st[k], e_x[k - 1, :, cols], preferred_element_type=F32)
            if i == na - 1:
                p_own[j] = p
                continue
            p_now[...] = p
            up = q > a
            has_in = (up & (a > 0)) | ((q < a) & (a < na - 1))

            @pl.when(has_in)
            def _():
                arrived(j, q)
                p_now[...] += gath[slot_at(j, q), :].astype(F32)

            gath[slot_at(j, q), :] = p_now[...].astype(BF16)

            @pl.when(up)
            def _():
                up_copy(j, q).start()

            @pl.when(q < a)
            def _():
                down_copy(j, q).start()

    def finish_chunk(j):
        @pl.when(a > 0)
        def _():
            arrived(j, a)
            p_own[j] += gath[slot_at(j, a), :].astype(F32)

        @pl.when(a < na - 1)
        def _():
            arrived(j, na)
            p_own[j] += gath[slot_at(j, na), :].astype(F32)

        for t in range(chunk // 128):
            at = pl.ds(pl.multiple_of(j * chunk + t * 128, 128), 128)
            m = jnp.broadcast_to(mass[:, at], (128, 128)).T
            m = jnp.concatenate([m] * (feats // 128), axis=1)
            out[at, :] = (p_own[j, t * 128:(t + 1) * 128, :] / m).astype(BF16)

    late = min(2, chunks - 1)

    @pl.loop(0, chunks)
    def _(j):
        send_chunk(j)

        @pl.when(j == late)
        def _():
            total = col_out[last]
            for k, c in enumerate(mass_copies, 1):
                c.wait()
                total = total + col_in[last, k]
            mass[...] = total

        @pl.when(j >= late)
        def _():
            finish_chunk(j - late)

    @pl.loop(chunks - late, chunks)
    def _(j):
        finish_chunk(j)

    @pl.loop(0, chunks)
    def _(j):
        for k in range(1, nb):
            share_copy(j, k).wait_send()
        for q in range(na):
            @pl.when(a < q)
            def _():
                up_copy(j, q).wait_send()

            @pl.when(a > q)
            def _():
                down_copy(j, q).wait_send()
    s_copy.wait()


def on_device(n, nc, embeddings, centroids):
    rows, width = embeddings.shape
    local_k, feats = centroids.shape
    target = rows * n / (local_k * nc)
    na = min(LINE, n)
    nb = n // na
    chunk = min(CHUNK, local_k)
    chunks = local_k // chunk
    vmem = pltpu.VMEM
    dma = pltpu.SemaphoreType.DMA
    hbm = pl.BlockSpec(memory_space=pl.ANY)
    return pl.pallas_call(
        functools.partial(step_kernel, n, nc, target, chunk),
        out_shape=(
            jax.ShapeDtypeStruct((rows, local_k), BF16),
            jax.ShapeDtypeStruct((local_k, feats), BF16),
        ),
        in_specs=[hbm, hbm],
        out_specs=(hbm, pl.BlockSpec(memory_space=pltpu.VMEM)),
        scratch_shapes=[
            vmem((rows, width), BF16),
            vmem((n * local_k, feats), BF16),
            vmem((rows, local_k), F32),
            vmem((8, local_k), F32),
            vmem((rows, 128), F32),
            vmem((rows, 128), F32),
            vmem((rows, local_k), BF16),
            vmem((nb - 1, rows, local_k), BF16),
            vmem((nb - 1, rows, na * feats), BF16),
            vmem((nb, chunk, rows), BF16),
            vmem((chunks, chunk, feats), F32),
            vmem((chunk, feats), F32),
            vmem((1, local_k), F32),
            vmem((1, local_k), F32),
            vmem((ROUNDS + 1, 1, local_k), F32),
            vmem((ROUNDS + 1, n, 1, local_k), F32),
            vmem((ROUNDS, rows // 128, 128), F32),
            vmem((ROUNDS, nc, rows // 128, 128), F32),
            dma((2,)),
            dma((n, 4, PIECES)),
            dma((n, PIECES)),
            dma((ROUNDS + 1, n)),
            dma((ROUNDS + 1, n)),
            dma((ROUNDS, nc)),
            dma((ROUNDS, nc)),
            dma((nb, na)),
            dma((nb, na)),
            dma((nb, nc)),
            dma((nb, nc)),
            dma((2, PIECES)),
            dma((chunks, nb)),
            dma((chunks, nb)),
            dma((chunks, na)),
            dma((chunks, na + 1)),
        ],
        compiler_params=pltpu.CompilerParams(
            collective_id=0, has_side_effects=True, vmem_limit_bytes=60 * 2**20
        ),
        cost_estimate=pl.CostEstimate(
            flops=4 * rows * width * local_k, bytes_accessed=48 * 2**20, transcendentals=rows * local_k
        ),
    )(embeddings, centroids)


def solution(mesh):
    in_specs = (P("dp", None), P("cent", "dp"))
    out_specs = (P("dp", "cent"), P("cent", "dp"))
    return jax.shard_map(
        functools.partial(on_device, mesh.shape["dp"], mesh.shape["cent"]),
        mesh=mesh, in_specs=in_specs, out_specs=out_specs, check_vma=False,
    )
```

```python
import functools

import jax
import jax.numpy as jnp
from jax import lax
from jax.experimental import pallas as pl
from jax.experimental.pallas import tpu as pltpu
from jax.sharding import PartitionSpec as P

ROUNDS = 3
LINE = 4
PIECES = 4
CHUNK = 256
DETOUR = 3
MESH = pl.DeviceIdType.MESH
F32 = jnp.float32
BF16 = jnp.bfloat16


def detour(a, na):
    if isinstance(a, int):
        return a + 1 if a < na // 2 else a - 1
    return jnp.where(a < na // 2, a + 1, a - 1)


def arrival_order(n, na, nb):
    table = []
    for me in range(n):
        a, b = divmod(me, nb)

        def key(s):
            da, db = abs(s // nb - a), abs(s % nb - b)
            late = nb == 2 and db > 0 and s // nb == detour(a, na)
            return (da + 1.2 * db + (10 if late else 0), s)

        table.append(sorted(range(n), key=key))
    return table


def pick(me, values):
    out = jnp.int32(values[0])
    for i, v in enumerate(values[1:], 1):
        out = jnp.where(me == i, jnp.int32(v), out)
    return out


def step_kernel(
    n, nc, target, chunk, emb, cent, shares, out, e_v, gath, w, sq, pr, rexp,
    s_v, s_x, e_x, st, p_own, p_now, mass, col_now, col_out, col_in, row_out, row_in, loc_sem, snd, rcv, csnd, crcv, rsnd, rrcv,
    esnd, ercv, fsnd, frcv, dsnd, xsnd, xrcv, snd2, rcv2,
):
    me = lax.axis_index("dp")
    mc = lax.axis_index("cent")
    na = min(LINE, n)
    nb = n // na
    a, b = me // nb, me % nb
    rows = e_v.shape[0]
    local_k, feats = cent.shape
    piece = local_k // PIECES
    tile = min(256, piece)
    lanes = local_k // 128

    barrier = pltpu.get_barrier_semaphore()
    for k in range(1, n):
        pl.semaphore_signal(barrier, inc=1, device_id={"dp": lax.rem(me + k, n)}, device_id_type=MESH)
    for k in range(1, nc):
        pl.semaphore_signal(barrier, inc=1, device_id={"cent": lax.rem(mc + k, nc)}, device_id_type=MESH)
    pl.semaphore_wait(barrier, n - 1 + nc - 1)

    order = arrival_order(n, na, nb)

    def sends(e, src, h):
        sa, sb = src // nb, src % nb
        da, db = sa - a, sb - b
        dst = gath.at[pl.ds(pl.multiple_of(src * local_k + h * piece, piece), piece)]
        ref = cent.at[pl.ds(pl.multiple_of(h * piece, piece), piece)] if e == 0 else dst
        across = jnp.bool_(True)
        if nb == 2:
            across = jnp.logical_not((h < DETOUR) & (sa == detour(a, na)))
        conds = (
            ((db == 0) & (da <= 0) & (a < na - 1), me + nb),
            ((db == 0) & (da >= 0) & (a > 0), me - nb),
            ((db <= 0) & (b < nb - 1) & across, me + 1),
            ((db >= 0) & (b > 0) & across, me - 1),
        )
        out = []
        for i, (cond, to) in enumerate(conds):
            out.append((cond, pltpu.make_async_remote_copy(
                src_ref=ref, dst_ref=dst, send_sem=snd.at[e, i, h], recv_sem=rcv.at[src, h],
                device_id={"dp": to}, device_id_type=MESH)))
        return out

    def detour_sends(h):
        src = a * nb + 1 - b
        ref = gath.at[pl.ds(pl.multiple_of(src * local_k + h * piece, piece), piece)]
        conds = (
            ((a < na - 1) & (detour(a + 1, na) == a), me + nb),
            ((a > 0) & (detour(a - 1, na) == a), me - nb),
        )
        return [(cond, pltpu.make_async_remote_copy(
            src_ref=ref, dst_ref=ref, send_sem=dsnd.at[i, h], recv_sem=rcv.at[src, h],
            device_id={"dp": to}, device_id_type=MESH)) for i, (cond, to) in enumerate(conds)]

    for h in range(PIECES):
        for cond, copy in sends(0, me, h):
            @pl.when(cond)
            def _():
                copy.start()
    part_rows = rows // nc
    mine = pl.ds(pl.multiple_of(mc * part_rows, part_rows), part_rows)
    e_copies, f_copies = [], []
    for k in range(1, nb):
        b2 = lax.rem(b + k, nb)
        for q in range(na):
            cols = pl.ds(pl.multiple_of((q * nb + b2) * feats, feats), feats)
            c = pltpu.make_async_remote_copy(
                src_ref=emb.at[mine, cols], dst_ref=e_x.at[k - 1, mine, pl.ds(q * feats, feats)],
                send_sem=esnd.at[k, q], recv_sem=ercv.at[k, q],
                device_id={"dp": a * nb + b2}, device_id_type=MESH)
            c.start()
            e_copies.append(c)
        for m in range(1, nc):
            f_copies.append(pltpu.make_async_remote_copy(
                src_ref=e_x.at[k - 1, mine], dst_ref=e_x.at[k - 1, mine],
                send_sem=fsnd.at[k, m], recv_sem=frcv.at[k, m],
                device_id={"cent": lax.rem(mc + m, nc)}, device_id_type=MESH))

    e_copy = pltpu.make_async_copy(emb, e_v, loc_sem.at[0])
    e_copy.start()
    own = pltpu.make_async_copy(
        cent, gath.at[pl.ds(pl.multiple_of(me * local_k, local_k), local_k)], loc_sem.at[1])
    own.start()
    e_copy.wait()

    @pl.loop(0, rows // 16)
    def _(i):
        at = pl.ds(pl.multiple_of(i * 16, 16), 16)
        x = e_v[at, :].astype(F32)
        s = jnp.sum(x * x, axis=1, keepdims=True)
        e_v[at, :] = (x * lax.rsqrt(s + 1e-06)).astype(BF16)

    own.wait()
    sq[...] = jnp.zeros_like(sq)
    nt = (((1,), (1,)), ((), ()))

    def narrow(x):
        parts = [x[:, t * 128:(t + 1) * 128] for t in range(x.shape[1] // 128)]
        while len(parts) > 1:
            half = [p + q for p, q in zip(parts[::2], parts[1::2])]
            parts = half + parts[len(half) * 2:]
        return parts[0]

    def source(e):
        return me if e == 0 else pick(me, [order[d][e] for d in range(n)])

    def take(e, h):
        src = source(e)
        fcols = pl.ds(pl.multiple_of(src * feats, feats), feats)
        if e > 0:
            outs = sends(e, src, h)
            outs[0][1].wait_recv()
            for cond, copy in outs:
                @pl.when(cond)
                def _():
                    copy.start()

        @pl.loop(0, piece // tile)
        def _(t):
            k0 = pl.multiple_of(h * piece + t * tile, tile)
            block = gath[pl.ds(pl.multiple_of(src * local_k + k0, tile), tile), :]
            part = lax.dot_general(e_v[:, fcols], block, nt, preferred_element_type=F32)
            if e == 0:
                w[:, pl.ds(k0, tile)] = part
            else:
                w[:, pl.ds(k0, tile)] += part
            bf = block.astype(F32)
            fold = narrow(bf * bf)
            for u in range(tile // 128):
                turned = fold[u * 128:(u + 1) * 128].T
                eights = turned[:8]
                for v in range(1, 16):
                    eights = eights + turned[v * 8:(v + 1) * 8]
                sq[:, pl.ds(pl.multiple_of(k0 + u * 128, 128), 128)] += eights

    for e in range(n - 1):
        if e < n - 2:
            @pl.loop(0, PIECES)
            def _(h):
                take(e, h)
        else:
            @pl.loop(0, PIECES)
            def _(h):
                take(e, h)
                take(e + 1, lax.rem(h + DETOUR, PIECES))

        if e == n // 2 - 1:
            for c in e_copies:
                c.wait()
            for c in f_copies:
                c.start()
        if nb == 2 and e == n // 2 + 1:
            for h in range(DETOUR):
                for cond, copy in detour_sends(h):
                    @pl.when(cond)
                    def _():
                        copy.start()

    for e in range(n):
        src = me if e == 0 else pick(me, [order[d][e] for d in range(n)])
        for h in range(PIECES):
            for cond, copy in sends(e, src, h):
                @pl.when(cond)
                def _():
                    copy.wait_send()
    if nb == 2:
        for h in range(DETOUR):
            for cond, copy in detour_sends(h):
                @pl.when(cond)
                def _():
                    copy.wait_send()

    for c in f_copies:
        c.wait()
    e_copy.start()

    def col_copies(r):
        return [pltpu.make_async_remote_copy(
            src_ref=col_out.at[r], dst_ref=col_in.at[r, k], send_sem=csnd.at[r, k], recv_sem=crcv.at[r, k],
            device_id={"dp": lax.rem(me + k, n)}, device_id_type=MESH) for k in range(1, n)]

    def exchange_cols(r, part8):
        col_out[r] = jnp.sum(part8, axis=0, keepdims=True)
        copies = col_copies(r)
        for c in copies:
            c.start()
        total = col_out[r]
        for k, c in enumerate(copies, 1):
            c.wait()
            total = total + col_in[r, k]
        return total

    def exchange_rows(r):
        for k in range(rows // 128):
            block = pr[k * 128:(k + 1) * 128, :]
            row_out[r, k:k + 1, :] = jnp.sum(block.T, axis=0, keepdims=True)
        copies = []
        for k in range(1, nc):
            c = pltpu.make_async_remote_copy(
                src_ref=row_out.at[r], dst_ref=row_in.at[r, k], send_sem=rsnd.at[r, k], recv_sem=rrcv.at[r, k],
                device_id={"cent": lax.rem(mc + k, nc)}, device_id_type=MESH)
            c.start()
            copies.append(c)
        total = row_out[r]
        for k, c in enumerate(copies, 1):
            c.wait()
            total = total + row_in[r, k]
        inv = 1.0 / total
        for k in range(rows // 128):
            rexp[k * 128:(k + 1) * 128, :] = jnp.broadcast_to(inv[k:k + 1, :], (128, 128)).T

    def wide(x):
        return jnp.concatenate([x] * lanes, axis=1)

    scale8 = jnp.broadcast_to(
        lax.rsqrt(jnp.sum(sq[...], axis=0, keepdims=True) + 1e-06) * 20.0, (8, local_k))
    zero8 = jnp.zeros((8, local_k), F32)

    def exp_pass(i, acc):
        at = pl.ds(pl.multiple_of(i * 8, 8), 8)
        x = jnp.exp(w[at, :] * scale8)
        w[at, :] = x
        return acc + x

    part8 = lax.fori_loop(0, rows // 8, exp_pass, zero8, unroll=4)
    for r in range(ROUNDS):
        if r > 0:
            def col_pass(i, acc):
                at = pl.ds(pl.multiple_of(i * 8, 8), 8)
                return acc + w[at, :] * wide(rexp[at, :])

            part8 = lax.fori_loop(0, rows // 8, col_pass, zero8, unroll=4)
        c8 = jnp.broadcast_to(target / exchange_cols(r, part8), (8, local_k))

        def row_pass(i, _):
            at = pl.ds(pl.multiple_of(i * 8, 8), 8)
            pr[at, :] = narrow(w[at, :] * c8)
            return 0

        lax.fori_loop(0, rows // 8, row_pass, 0, unroll=4)
        exchange_rows(r)

    chunks = local_k // chunk

    def span(j):
        return pl.ds(pl.multiple_of(j * chunk, chunk), chunk)

    def share_copy(j, k):
        return pltpu.make_async_remote_copy(
            src_ref=s_v.at[:, span(j)], dst_ref=s_x.at[k - 1, :, span(j)],
            send_sem=xsnd.at[j, k], recv_sem=xrcv.at[j, k],
            device_id={"dp": a * nb + lax.rem(b + k, nb)}, device_id_type=MESH)

    col_now[...] = c8[:1]
    last = ROUNDS

    @pl.loop(0, chunks)
    def _(j):
        c16 = jnp.broadcast_to(col_now[:, span(j)], (16, chunk))

        def share_pass(i, acc):
            at = pl.ds(pl.multiple_of(i * 16, 16), 16)
            r = rexp[at, :]
            x = (w[at, span(j)] * jnp.concatenate([r] * (chunk // 128), axis=1) * c16).astype(BF16)
            s_v[at, span(j)] = x
            x = x.astype(F32)
            return acc + (x[:8] + x[8:])

        part = lax.fori_loop(0, rows // 16, share_pass, jnp.zeros((8, chunk), F32), unroll=4)
        col_out[last, :, span(j)] = jnp.sum(part, axis=0, keepdims=True)

        @pl.when(j == 0)
        def _():
            for k in range(1, nb):
                share_copy(j, k).start()

    mass_copies = col_copies(last)
    for c in mass_copies:
        c.start()

    @pl.loop(1, chunks)
    def _(j):
        for k in range(1, nb):
            share_copy(j, k).start()

    s_copy = pltpu.make_async_copy(s_v, shares, loc_sem.at[1])
    s_copy.start()
    e_copy.wait()

    def slot_at(j, q):
        return pl.ds(pl.multiple_of((j * (na + 1) + q) * chunk, chunk), chunk)

    def slot(j, q):
        return gath.at[slot_at(j, q)]

    far_first = [sorted(range(na), key=lambda q: (-abs(q - m), q)) for m in range(na)]

    def up_copy(j, q):
        return pltpu.make_async_remote_copy(
            src_ref=slot(j, q), dst_ref=slot(j, q), send_sem=snd2.at[j, q], recv_sem=rcv2.at[j, q],
            device_id={"dp": me + nb}, device_id_type=MESH)

    def down_copy(j, q):
        to = jnp.where(q == a - 1, na, q)
        return pltpu.make_async_remote_copy(
            src_ref=slot(j, q), dst_ref=slot(j, to), send_sem=snd2.at[j, q], recv_sem=rcv2.at[j, to],
            device_id={"dp": me - nb}, device_id_type=MESH)

    def arrived(j, q):
        pltpu.make_async_remote_copy(
            src_ref=slot(j, q), dst_ref=slot(j, q), send_sem=snd2.at[j, 0], recv_sem=rcv2.at[j, q],
            device_id={"dp": me}, device_id_type=MESH).wait_recv()

    def send_chunk(j):
        for k in range(1, nb):
            share_copy(j, k).wait_recv()
        st[0] = s_v[:, span(j)].T
        for k in range(1, nb):
            st[k] = s_x[k - 1, :, span(j)].T
        for i in range(na):
            q = pick(a, [far_first[m][i] for m in range(na)])
            cols = pl.ds(pl.multiple_of(q * feats, feats), feats)
            own_cols = pl.ds(pl.multiple_of((q * nb + b) * feats, feats), feats)
            p = jnp.dot(st[0], e_v[:, own_cols], preferred_element_type=F32)
            for k in range(1, nb):
                p = p + jnp.dot(st[k], e_x[k - 1, :, cols], preferred_element_type=F32)
            if i == na - 1:
                p_own[j] = p
                continue
            p_now[...] = p
            up = q > a
            has_in = (up & (a > 0)) | ((q < a) & (a < na - 1))

            @pl.when(has_in)
            def _():
                arrived(j, q)
                p_now[...] += gath[slot_at(j, q), :].astype(F32)

            gath[slot_at(j, q), :] = p_now[...].astype(BF16)

            @pl.when(up)
            def _():
                up_copy(j, q).start()

            @pl.when(q < a)
            def _():
                down_copy(j, q).start()

    def finish_chunk(j):
        @pl.when(a > 0)
        def _():
            arrived(j, a)
            p_own[j] += gath[slot_at(j, a), :].astype(F32)

        @pl.when(a < na - 1)
        def _():
            arrived(j, na)
            p_own[j] += gath[slot_at(j, na), :].astype(F32)

        for t in range(chunk // 128):
            at = pl.ds(pl.multiple_of(j * chunk + t * 128, 128), 128)
            m = jnp.broadcast_to(mass[:, at], (128, 128)).T
            m = jnp.concatenate([m] * (feats // 128), axis=1)
            out[at, :] = (p_own[j, t * 128:(t + 1) * 128, :] / m).astype(BF16)

    late = min(2, chunks - 1)

    @pl.loop(0, chunks)
    def _(j):
        send_chunk(j)

        @pl.when(j == late)
        def _():
            total = col_out[last]
            for k, c in enumerate(mass_copies, 1):
                c.wait()
                total = total + col_in[last, k]
            mass[...] = total

        @pl.when(j >= late)
        def _():
            finish_chunk(j - late)

    @pl.loop(chunks - late, chunks)
    def _(j):
        finish_chunk(j)

    @pl.loop(0, chunks)
    def _(j):
        for k in range(1, nb):
            share_copy(j, k).wait_send()
        for q in range(na):
            @pl.when(a < q)
            def _():
                up_copy(j, q).wait_send()

            @pl.when(a > q)
            def _():
                down_copy(j, q).wait_send()
    s_copy.wait()


def on_device(n, nc, embeddings, centroids):
    rows, width = embeddings.shape
    local_k, feats = centroids.shape
    target = rows * n / (local_k * nc)
    na = min(LINE, n)
    nb = n // na
    chunk = min(CHUNK, local_k)
    chunks = local_k // chunk
    vmem = pltpu.VMEM
    dma = pltpu.SemaphoreType.DMA
    hbm = pl.BlockSpec(memory_space=pl.ANY)
    return pl.pallas_call(
        functools.partial(step_kernel, n, nc, target, chunk),
        out_shape=(
            jax.ShapeDtypeStruct((rows, local_k), BF16),
            jax.ShapeDtypeStruct((local_k, feats), BF16),
        ),
        in_specs=[hbm, hbm],
        out_specs=(hbm, pl.BlockSpec(memory_space=pltpu.VMEM)),
        scratch_shapes=[
            vmem((rows, width), BF16),
            vmem((n * local_k, feats), BF16),
            vmem((rows, local_k), F32),
            vmem((8, local_k), F32),
            vmem((rows, 128), F32),
            vmem((rows, 128), F32),
            vmem((rows, local_k), BF16),
            vmem((nb - 1, rows, local_k), BF16),
            vmem((nb - 1, rows, na * feats), BF16),
            vmem((nb, chunk, rows), BF16),
            vmem((chunks, chunk, feats), F32),
            vmem((chunk, feats), F32),
            vmem((1, local_k), F32),
            vmem((1, local_k), F32),
            vmem((ROUNDS + 1, 1, local_k), F32),
            vmem((ROUNDS + 1, n, 1, local_k), F32),
            vmem((ROUNDS, rows // 128, 128), F32),
            vmem((ROUNDS, nc, rows // 128, 128), F32),
            dma((2,)),
            dma((n, 4, PIECES)),
            dma((n, PIECES)),
            dma((ROUNDS + 1, n)),
            dma((ROUNDS + 1, n)),
            dma((ROUNDS, nc)),
            dma((ROUNDS, nc)),
            dma((nb, na)),
            dma((nb, na)),
            dma((nb, nc)),
            dma((nb, nc)),
            dma((2, PIECES)),
            dma((chunks, nb)),
            dma((chunks, nb)),
            dma((chunks, na)),
            dma((chunks, na + 1)),
        ],
        compiler_params=pltpu.CompilerParams(
            collective_id=0, has_side_effects=True, vmem_limit_bytes=60 * 2**20
        ),
        cost_estimate=pl.CostEstimate(
            flops=4 * rows * width * local_k, bytes_accessed=48 * 2**20, transcendentals=rows * local_k
        ),
    )(embeddings, centroids)


def solution(mesh):
    in_specs = (P("dp", None), P("cent", "dp"))
    out_specs = (P("dp", "cent"), P("cent", "dp"))
    return jax.shard_map(
        functools.partial(on_device, mesh.shape["dp"], mesh.shape["cent"]),
        mesh=mesh, in_specs=in_specs, out_specs=out_specs, check_vma=False,
    )
```

```python
import functools

import jax
import jax.numpy as jnp
from jax import lax
from jax.experimental import pallas as pl
from jax.experimental.pallas import tpu as pltpu
from jax.sharding import PartitionSpec as P

ROUNDS = 3
LINE = 4
PIECES = 4
CHUNK = 128
DETOUR = 3
MESH = pl.DeviceIdType.MESH
F32 = jnp.float32
BF16 = jnp.bfloat16


def detour(a, na):
    if isinstance(a, int):
        return a + 1 if a < na // 2 else a - 1
    return jnp.where(a < na // 2, a + 1, a - 1)


def arrival_order(n, na, nb):
    table = []
    for me in range(n):
        a, b = divmod(me, nb)

        def key(s):
            da, db = abs(s // nb - a), abs(s % nb - b)
            late = nb == 2 and db > 0 and s // nb == detour(a, na)
            return (da + 1.2 * db + (10 if late else 0), s)

        table.append(sorted(range(n), key=key))
    return table


def pick(me, values):
    out = jnp.int32(values[0])
    for i, v in enumerate(values[1:], 1):
        out = jnp.where(me == i, jnp.int32(v), out)
    return out


def step_kernel(
    n, nc, target, chunk, emb, cent, shares, out, e_v, gath, w, sq, pr, rexp,
    s_v, s_x, e_x, st, p_own, p_now, mass, col_now, col_out, col_in, row_out, row_in, loc_sem, snd, rcv, csnd, crcv, rsnd, rrcv,
    esnd, ercv, fsnd, frcv, dsnd, xsnd, xrcv, snd2, rcv2,
):
    me = lax.axis_index("dp")
    mc = lax.axis_index("cent")
    na = min(LINE, n)
    nb = n // na
    a, b = me // nb, me % nb
    rows = e_v.shape[0]
    local_k, feats = cent.shape
    piece = local_k // PIECES
    tile = min(256, piece)
    lanes = local_k // 128

    barrier = pltpu.get_barrier_semaphore()
    for k in range(1, n):
        pl.semaphore_signal(barrier, inc=1, device_id={"dp": lax.rem(me + k, n)}, device_id_type=MESH)
    for k in range(1, nc):
        pl.semaphore_signal(barrier, inc=1, device_id={"cent": lax.rem(mc + k, nc)}, device_id_type=MESH)
    pl.semaphore_wait(barrier, n - 1 + nc - 1)

    order = arrival_order(n, na, nb)

    def sends(e, src, h):
        sa, sb = src // nb, src % nb
        da, db = sa - a, sb - b
        dst = gath.at[pl.ds(pl.multiple_of(src * local_k + h * piece, piece), piece)]
        ref = cent.at[pl.ds(pl.multiple_of(h * piece, piece), piece)] if e == 0 else dst
        across = jnp.bool_(True)
        if nb == 2:
            across = jnp.logical_not((h < DETOUR) & (sa == detour(a, na)))
        conds = (
            ((db == 0) & (da <= 0) & (a < na - 1), me + nb),
            ((db == 0) & (da >= 0) & (a > 0), me - nb),
            ((db <= 0) & (b < nb - 1) & across, me + 1),
            ((db >= 0) & (b > 0) & across, me - 1),
        )
        out = []
        for i, (cond, to) in enumerate(conds):
            out.append((cond, pltpu.make_async_remote_copy(
                src_ref=ref, dst_ref=dst, send_sem=snd.at[e, i, h], recv_sem=rcv.at[src, h],
                device_id={"dp": to}, device_id_type=MESH)))
        return out

    def detour_sends(h):
        src = a * nb + 1 - b
        ref = gath.at[pl.ds(pl.multiple_of(src * local_k + h * piece, piece), piece)]
        conds = (
            ((a < na - 1) & (detour(a + 1, na) == a), me + nb),
            ((a > 0) & (detour(a - 1, na) == a), me - nb),
        )
        return [(cond, pltpu.make_async_remote_copy(
            src_ref=ref, dst_ref=ref, send_sem=dsnd.at[i, h], recv_sem=rcv.at[src, h],
            device_id={"dp": to}, device_id_type=MESH)) for i, (cond, to) in enumerate(conds)]

    for h in range(PIECES):
        for cond, copy in sends(0, me, h):
            @pl.when(cond)
            def _():
                copy.start()
    part_rows = rows // nc
    mine = pl.ds(pl.multiple_of(mc * part_rows, part_rows), part_rows)
    e_copies, f_copies = [], []
    for k in range(1, nb):
        b2 = lax.rem(b + k, nb)
        for q in range(na):
            cols = pl.ds(pl.multiple_of((q * nb + b2) * feats, feats), feats)
            c = pltpu.make_async_remote_copy(
                src_ref=emb.at[mine, cols], dst_ref=e_x.at[k - 1, mine, pl.ds(q * feats, feats)],
                send_sem=esnd.at[k, q], recv_sem=ercv.at[k, q],
                device_id={"dp": a * nb + b2}, device_id_type=MESH)
            c.start()
            e_copies.append(c)
        for m in range(1, nc):
            f_copies.append(pltpu.make_async_remote_copy(
                src_ref=e_x.at[k - 1, mine], dst_ref=e_x.at[k - 1, mine],
                send_sem=fsnd.at[k, m], recv_sem=frcv.at[k, m],
                device_id={"cent": lax.rem(mc + m, nc)}, device_id_type=MESH))

    e_copy = pltpu.make_async_copy(emb, e_v, loc_sem.at[0])
    e_copy.start()
    own = pltpu.make_async_copy(
        cent, gath.at[pl.ds(pl.multiple_of(me * local_k, local_k), local_k)], loc_sem.at[1])
    own.start()
    e_copy.wait()

    @pl.loop(0, rows // 16)
    def _(i):
        at = pl.ds(pl.multiple_of(i * 16, 16), 16)
        x = e_v[at, :].astype(F32)
        s = jnp.sum(x * x, axis=1, keepdims=True)
        e_v[at, :] = (x * lax.rsqrt(s + 1e-06)).astype(BF16)

    own.wait()
    sq[...] = jnp.zeros_like(sq)
    nt = (((1,), (1,)), ((), ()))

    def narrow(x):
        parts = [x[:, t * 128:(t + 1) * 128] for t in range(x.shape[1] // 128)]
        while len(parts) > 1:
            half = [p + q for p, q in zip(parts[::2], parts[1::2])]
            parts = half + parts[len(half) * 2:]
        return parts[0]

    def source(e):
        return me if e == 0 else pick(me, [order[d][e] for d in range(n)])

    def take(e, h):
        src = source(e)
        fcols = pl.ds(pl.multiple_of(src * feats, feats), feats)
        if e > 0:
            outs = sends(e, src, h)
            outs[0][1].wait_recv()
            for cond, copy in outs:
                @pl.when(cond)
                def _():
                    copy.start()

        @pl.loop(0, piece // tile)
        def _(t):
            k0 = pl.multiple_of(h * piece + t * tile, tile)
            block = gath[pl.ds(pl.multiple_of(src * local_k + k0, tile), tile), :]
            part = lax.dot_general(e_v[:, fcols], block, nt, preferred_element_type=F32)
            if e == 0:
                w[:, pl.ds(k0, tile)] = part
            else:
                w[:, pl.ds(k0, tile)] += part
            bf = block.astype(F32)
            fold = narrow(bf * bf)
            for u in range(tile // 128):
                turned = fold[u * 128:(u + 1) * 128].T
                eights = turned[:8]
                for v in range(1, 16):
                    eights = eights + turned[v * 8:(v + 1) * 8]
                sq[:, pl.ds(pl.multiple_of(k0 + u * 128, 128), 128)] += eights

    for e in range(n - 1):
        if e < n - 2:
            @pl.loop(0, PIECES)
            def _(h):
                take(e, h)
        else:
            @pl.loop(0, PIECES)
            def _(h):
                take(e, h)
                take(e + 1, lax.rem(h + DETOUR, PIECES))

        if e == n // 2 - 1:
            for c in e_copies:
                c.wait()
            for c in f_copies:
                c.start()
        if nb == 2 and e == n // 2 + 1:
            for h in range(DETOUR):
                for cond, copy in detour_sends(h):
                    @pl.when(cond)
                    def _():
                        copy.start()

    for e in range(n):
        src = me if e == 0 else pick(me, [order[d][e] for d in range(n)])
        for h in range(PIECES):
            for cond, copy in sends(e, src, h):
                @pl.when(cond)
                def _():
                    copy.wait_send()
    if nb == 2:
        for h in range(DETOUR):
            for cond, copy in detour_sends(h):
                @pl.when(cond)
                def _():
                    copy.wait_send()

    for c in f_copies:
        c.wait()
    e_copy.start()

    def col_copies(r):
        return [pltpu.make_async_remote_copy(
            src_ref=col_out.at[r], dst_ref=col_in.at[r, k], send_sem=csnd.at[r, k], recv_sem=crcv.at[r, k],
            device_id={"dp": lax.rem(me + k, n)}, device_id_type=MESH) for k in range(1, n)]

    def exchange_cols(r, part8):
        col_out[r] = jnp.sum(part8, axis=0, keepdims=True)
        copies = col_copies(r)
        for c in copies:
            c.start()
        total = col_out[r]
        for k, c in enumerate(copies, 1):
            c.wait()
            total = total + col_in[r, k]
        return total

    def exchange_rows(r):
        for k in range(rows // 128):
            block = pr[k * 128:(k + 1) * 128, :]
            row_out[r, k:k + 1, :] = jnp.sum(block.T, axis=0, keepdims=True)
        copies = []
        for k in range(1, nc):
            c = pltpu.make_async_remote_copy(
                src_ref=row_out.at[r], dst_ref=row_in.at[r, k], send_sem=rsnd.at[r, k], recv_sem=rrcv.at[r, k],
                device_id={"cent": lax.rem(mc + k, nc)}, device_id_type=MESH)
            c.start()
            copies.append(c)
        total = row_out[r]
        for k, c in enumerate(copies, 1):
            c.wait()
            total = total + row_in[r, k]
        inv = 1.0 / total
        for k in range(rows // 128):
            rexp[k * 128:(k + 1) * 128, :] = jnp.broadcast_to(inv[k:k + 1, :], (128, 128)).T

    def wide(x):
        return jnp.concatenate([x] * lanes, axis=1)

    scale8 = jnp.broadcast_to(
        lax.rsqrt(jnp.sum(sq[...], axis=0, keepdims=True) + 1e-06) * 20.0, (8, local_k))
    zero8 = jnp.zeros((8, local_k), F32)

    def exp_pass(i, acc):
        at = pl.ds(pl.multiple_of(i * 8, 8), 8)
        x = jnp.exp(w[at, :] * scale8)
        w[at, :] = x
        return acc + x

    part8 = lax.fori_loop(0, rows // 8, exp_pass, zero8, unroll=4)
    for r in range(ROUNDS):
        if r > 0:
            def col_pass(i, acc):
                at = pl.ds(pl.multiple_of(i * 8, 8), 8)
                return acc + w[at, :] * wide(rexp[at, :])

            part8 = lax.fori_loop(0, rows // 8, col_pass, zero8, unroll=4)
        c8 = jnp.broadcast_to(target / exchange_cols(r, part8), (8, local_k))

        def row_pass(i, _):
            at = pl.ds(pl.multiple_of(i * 8, 8), 8)
            pr[at, :] = narrow(w[at, :] * c8)
            return 0

        lax.fori_loop(0, rows // 8, row_pass, 0, unroll=4)
        exchange_rows(r)

    chunks = local_k // chunk

    def span(j):
        return pl.ds(pl.multiple_of(j * chunk, chunk), chunk)

    def share_copy(j, k):
        return pltpu.make_async_remote_copy(
            src_ref=s_v.at[:, span(j)], dst_ref=s_x.at[k - 1, :, span(j)],
            send_sem=xsnd.at[j, k], recv_sem=xrcv.at[j, k],
            device_id={"dp": a * nb + lax.rem(b + k, nb)}, device_id_type=MESH)

    col_now[...] = c8[:1]
    last = ROUNDS

    @pl.loop(0, chunks)
    def _(j):
        c16 = jnp.broadcast_to(col_now[:, span(j)], (16, chunk))

        def share_pass(i, acc):
            at = pl.ds(pl.multiple_of(i * 16, 16), 16)
            r = rexp[at, :]
            x = (w[at, span(j)] * jnp.concatenate([r] * (chunk // 128), axis=1) * c16).astype(BF16)
            s_v[at, span(j)] = x
            x = x.astype(F32)
            return acc + (x[:8] + x[8:])

        part = lax.fori_loop(0, rows // 16, share_pass, jnp.zeros((8, chunk), F32), unroll=4)
        col_out[last, :, span(j)] = jnp.sum(part, axis=0, keepdims=True)

        @pl.when(j == 0)
        def _():
            for k in range(1, nb):
                share_copy(j, k).start()

    mass_copies = col_copies(last)
    for c in mass_copies:
        c.start()

    @pl.loop(1, chunks)
    def _(j):
        for k in range(1, nb):
            share_copy(j, k).start()

    s_copy = pltpu.make_async_copy(s_v, shares, loc_sem.at[1])
    s_copy.start()
    e_copy.wait()

    def slot_at(j, q):
        return pl.ds(pl.multiple_of((j * (na + 1) + q) * chunk, chunk), chunk)

    def slot(j, q):
        return gath.at[slot_at(j, q)]

    far_first = [sorted(range(na), key=lambda q: (-abs(q - m), q)) for m in range(na)]

    def up_copy(j, q):
        return pltpu.make_async_remote_copy(
            src_ref=slot(j, q), dst_ref=slot(j, q), send_sem=snd2.at[j, q], recv_sem=rcv2.at[j, q],
            device_id={"dp": me + nb}, device_id_type=MESH)

    def down_copy(j, q):
        to = jnp.where(q == a - 1, na, q)
        return pltpu.make_async_remote_copy(
            src_ref=slot(j, q), dst_ref=slot(j, to), send_sem=snd2.at[j, q], recv_sem=rcv2.at[j, to],
            device_id={"dp": me - nb}, device_id_type=MESH)

    def arrived(j, q):
        pltpu.make_async_remote_copy(
            src_ref=slot(j, q), dst_ref=slot(j, q), send_sem=snd2.at[j, 0], recv_sem=rcv2.at[j, q],
            device_id={"dp": me}, device_id_type=MESH).wait_recv()

    def send_chunk(j):
        for k in range(1, nb):
            share_copy(j, k).wait_recv()
        st[0] = s_v[:, span(j)].T
        for k in range(1, nb):
            st[k] = s_x[k - 1, :, span(j)].T
        for i in range(na):
            q = pick(a, [far_first[m][i] for m in range(na)])
            cols = pl.ds(pl.multiple_of(q * feats, feats), feats)
            own_cols = pl.ds(pl.multiple_of((q * nb + b) * feats, feats), feats)
            p = jnp.dot(st[0], e_v[:, own_cols], preferred_element_type=F32)
            for k in range(1, nb):
                p = p + jnp.dot(st[k], e_x[k - 1, :, cols], preferred_element_type=F32)
            if i == na - 1:
                p_own[j] = p
                continue
            p_now[...] = p
            up = q > a
            has_in = (up & (a > 0)) | ((q < a) & (a < na - 1))

            @pl.when(has_in)
            def _():
                arrived(j, q)
                p_now[...] += gath[slot_at(j, q), :].astype(F32)

            gath[slot_at(j, q), :] = p_now[...].astype(BF16)

            @pl.when(up)
            def _():
                up_copy(j, q).start()

            @pl.when(q < a)
            def _():
                down_copy(j, q).start()

    def finish_chunk(j):
        @pl.when(a > 0)
        def _():
            arrived(j, a)
            p_own[j] += gath[slot_at(j, a), :].astype(F32)

        @pl.when(a < na - 1)
        def _():
            arrived(j, na)
            p_own[j] += gath[slot_at(j, na), :].astype(F32)

        for t in range(chunk // 128):
            at = pl.ds(pl.multiple_of(j * chunk + t * 128, 128), 128)
            m = jnp.broadcast_to(mass[:, at], (128, 128)).T
            m = jnp.concatenate([m] * (feats // 128), axis=1)
            out[at, :] = (p_own[j, t * 128:(t + 1) * 128, :] / m).astype(BF16)

    late = min(2, chunks - 1)

    @pl.loop(0, chunks)
    def _(j):
        send_chunk(j)

        @pl.when(j == late)
        def _():
            total = col_out[last]
            for k, c in enumerate(mass_copies, 1):
                c.wait()
                total = total + col_in[last, k]
            mass[...] = total

        @pl.when(j >= late)
        def _():
            finish_chunk(j - late)

    @pl.loop(chunks - late, chunks)
    def _(j):
        finish_chunk(j)

    @pl.loop(0, chunks)
    def _(j):
        for k in range(1, nb):
            share_copy(j, k).wait_send()
        for q in range(na):
            @pl.when(a < q)
            def _():
                up_copy(j, q).wait_send()

            @pl.when(a > q)
            def _():
                down_copy(j, q).wait_send()
    s_copy.wait()


def on_device(n, nc, embeddings, centroids):
    rows, width = embeddings.shape
    local_k, feats = centroids.shape
    target = rows * n / (local_k * nc)
    na = min(LINE, n)
    nb = n // na
    chunk = min(CHUNK, local_k)
    chunks = local_k // chunk
    vmem = pltpu.VMEM
    dma = pltpu.SemaphoreType.DMA
    hbm = pl.BlockSpec(memory_space=pl.ANY)
    return pl.pallas_call(
        functools.partial(step_kernel, n, nc, target, chunk),
        out_shape=(
            jax.ShapeDtypeStruct((rows, local_k), BF16),
            jax.ShapeDtypeStruct((local_k, feats), BF16),
        ),
        in_specs=[hbm, hbm],
        out_specs=(hbm, pl.BlockSpec(memory_space=pltpu.VMEM)),
        scratch_shapes=[
            vmem((rows, width), BF16),
            vmem((n * local_k, feats), BF16),
            vmem((rows, local_k), F32),
            vmem((8, local_k), F32),
            vmem((rows, 128), F32),
            vmem((rows, 128), F32),
            vmem((rows, local_k), BF16),
            vmem((nb - 1, rows, local_k), BF16),
            vmem((nb - 1, rows, na * feats), BF16),
            vmem((nb, chunk, rows), BF16),
            vmem((chunks, chunk, feats), F32),
            vmem((chunk, feats), F32),
            vmem((1, local_k), F32),
            vmem((1, local_k), F32),
            vmem((ROUNDS + 1, 1, local_k), F32),
            vmem((ROUNDS + 1, n, 1, local_k), F32),
            vmem((ROUNDS, rows // 128, 128), F32),
            vmem((ROUNDS, nc, rows // 128, 128), F32),
            dma((2,)),
            dma((n, 4, PIECES)),
            dma((n, PIECES)),
            dma((ROUNDS + 1, n)),
            dma((ROUNDS + 1, n)),
            dma((ROUNDS, nc)),
            dma((ROUNDS, nc)),
            dma((nb, na)),
            dma((nb, na)),
            dma((nb, nc)),
            dma((nb, nc)),
            dma((2, PIECES)),
            dma((chunks, nb)),
            dma((chunks, nb)),
            dma((chunks, na)),
            dma((chunks, na + 1)),
        ],
        compiler_params=pltpu.CompilerParams(
            collective_id=0, has_side_effects=True, vmem_limit_bytes=60 * 2**20
        ),
        cost_estimate=pl.CostEstimate(
            flops=4 * rows * width * local_k, bytes_accessed=48 * 2**20, transcendentals=rows * local_k
        ),
    )(embeddings, centroids)


def solution(mesh):
    in_specs = (P("dp", None), P("cent", "dp"))
    out_specs = (P("dp", "cent"), P("cent", "dp"))
    return jax.shard_map(
        functools.partial(on_device, mesh.shape["dp"], mesh.shape["cent"]),
        mesh=mesh, in_specs=in_specs, out_specs=out_specs, check_vma=False,
    )
```
